512 devices in a mesh: dp: 32 (over z, x), head: 16 (over y, core).
Axes of the slice: x: 4, y: 8, z: 8, core: 2. Of those that a mesh axis runs over, the one named last changes fastest.
Arguments:
- inputs: bfloat16 [16384, 4608], P('dp', 'head'), may hold values from -6 to 6
- w_query: bfloat16 [4608, 4096], P('dp', 'head'), may hold values from -0.3125 to 0.3125
- w_key: bfloat16 [4608, 2048], P('dp', 'head'), may hold values from -0.3125 to 0.3125
- w_value: bfloat16 [4608, 2048], P('dp', 'head'), may hold values from -0.09375 to 0.09375
- cotangent: bfloat16 [16384, 4096], P('dp', 'head'), may hold values from -150 to 150
- lengths: int32 [64], P('dp'), may hold values from 32 to 256, as said below
- sampled: int32 [64], P('dp'), may hold values 0 or 1
- step: int32 [1], replicated, may hold values from 1 to 15
- tree_noise: float32 [4, 2, 4608, 2048], P(None, None, 'dp', 'head'), may hold values from -1.75 to 1.75
Outputs:
- noisy_key_gradient: float32 [4608, 2048], P('dp', 'head')
- noisy_value_gradient: float32 [4608, 2048], P('dp', 'head')
The draws below stay inside these ranges and needn't reach their ends.
Inputs may be any that keep to these rules, and one draw needn't show every extreme that they name: `lengths`: every draw has a sequence of exactly 256 and one of exactly 32 tokens.
All inputs are finite; a program needn't handle non-finite values. No bound on the sum of `sampled` on one device may be relied on, other than what follows from the above.
Results may differ from the reference program's by a relative error of at most 0.017.
Values may be sent and summed in bfloat16 or wider, within the bound.
No kernel may reach another device: no remote copies, remote signals or barrier semaphores. Data moves between devices by JAX's collectives and lax.ppermute only.
A program may use at most 64 MiB of HBM per device.

```python
import math
import jax
import jax.numpy as jnp
from jax import lax

D = 4608
H = 32
KV = 16
HD = 128
L = 256
SEQ_DEV = 2
LEVELS = 4
SEQS = 64
N_DP = 32


def draw_inputs(key, part):
    key = jax.random.fold_in(key, 13)
    keys = jax.random.split(key, 2)
    own = jnp.clip(jax.random.normal(keys[0], (SEQS, L, D), jnp.float32), -4.0, 4.0)
    common = jnp.clip(jax.random.normal(keys[1], (SEQS, 1, D), jnp.float32), -4.0, 4.0)
    values = 0.55 * own + 0.84 * common
    return values.reshape(SEQS * L, D).astype(jnp.bfloat16)


def draw_cotangent(key, part):
    key = jax.random.fold_in(key, 11)
    keys = jax.random.split(key, 4)
    seq_scale = jnp.exp(jax.random.uniform(keys[0], (SEQS, 1, 1, 1), jnp.float32, math.log(0.1), math.log(10.0)))
    row_scale = jax.random.uniform(keys[1], (SEQS, L, 1, 1), jnp.float32, 0.5, 1.5)
    head_scale = jnp.exp(jax.random.uniform(keys[2], (1, 1, H, 1), jnp.float32, math.log(0.4), math.log(2.5)))
    base = jnp.clip(jax.random.normal(keys[3], (SEQS, L, H, HD), jnp.float32), -4.0, 4.0)
    values = base * seq_scale * row_scale * head_scale
    return values.reshape(SEQS * L, H * HD).astype(jnp.bfloat16)


def draw_lengths(key, part):
    key = jax.random.fold_in(key, 12)
    keys = jax.random.split(key, 3)
    shortest = L // 8
    drawn = jax.random.randint(keys[0], (SEQS,), shortest, L + 1)
    first = jax.random.randint(keys[1], (), 0, SEQS)
    second = (first + 1 + jax.random.randint(keys[2], (), 0, SEQS - 1)) % SEQS
    drawn = drawn.at[first].set(L).at[second].set(shortest)
    return drawn.astype(jnp.int32)


def place_ends(values, key, least, top_value):
    extent = values.shape
    place = [jax.random.randint(jax.random.fold_in(key, axis), (), 0, extent[axis]) for axis in range(len(extent))]
    values = values.at[tuple(place)].set(least)
    longest = extent.index(max(extent))
    place[longest] = (place[longest] + 1) % extent[longest]
    return values.at[tuple(place)].set(top_value)


def steps_of(key, extent, cuts, least, top_value):
    level, own = 1.0, jax.random.fold_in(key, 6)
    for dim, shards_of in cuts:
        heights = jnp.exp(jax.random.uniform(jax.random.fold_in(own, dim), (shards_of,), jnp.float32, least / len(cuts), top_value / len(cuts)))
        level = level * jnp.repeat(heights, extent[dim] // shards_of).reshape([-1 if axis == dim else 1 for axis in range(len(extent))])
    return level


def scatter_about(rng, shape, deviation, reach, cuts=(), held_as=jnp.bfloat16):
    array = deviation * jax.random.normal(rng, shape, jnp.float32)
    if cuts:
        array = array * steps_of(rng, shape, cuts, -0.22, 0.18)
    return jnp.clip(array, -reach, reach).astype(held_as)


def setup_inputs(seed: int = 0) -> dict:
    arg_keys = jax.random.split(jax.random.key(seed), 10)
    inputs = draw_inputs(jax.random.fold_in(arg_keys[9], 71), 0)
    w_query = scatter_about(arg_keys[1], (D, H * HD), (HD * D // (12 * (D // H))) ** -0.5, 0.3125, ((0, 32), (1, 16)))
    w_key = scatter_about(arg_keys[2], (D, KV * HD), (HD * D // (12 * (D // H))) ** -0.5, 0.3125, ((0, 32), (1, 16)))
    w_value = scatter_about(arg_keys[3], (D, KV * HD), D ** -0.5, 0.09375, ((0, 32), (1, 16)))
    cotangent = draw_cotangent(jax.random.fold_in(arg_keys[9], 71), 0)
    lengths = draw_lengths(jax.random.fold_in(arg_keys[9], 71), 0)
    sampled = place_ends((jax.random.randint(arg_keys[6], (SEQS,), 0, 20) < 17).astype(jnp.int32), jax.random.fold_in(arg_keys[6], 1), 0, 1)
    step = jax.random.randint(arg_keys[7], (1,), 1, 2 ** LEVELS).astype(jnp.int32)
    tree_noise = scatter_about(arg_keys[8], (LEVELS, 2, D, KV * HD), 0.3, 1.75, ((2, 32), (3, 16)), jnp.float32)
    return {"inputs": inputs, "w_query": w_query, "w_key": w_key, "w_value": w_value, "cotangent": cotangent, "lengths": lengths, "sampled": sampled, "step": step, "tree_noise": tree_noise}


cap_value = 50.0

def rounded(value):
    return lax.optimization_barrier(value.astype(jnp.bfloat16)).astype(jnp.float32)

def rope_tables(length, dim):
    half = dim // 2
    freq = 10000.0 ** (-(jnp.arange(half, dtype=jnp.float32) * (2.0 / dim)))
    angle = jnp.arange(length, dtype=jnp.float32)[:, None] * freq[None, :]
    cosine = jnp.cos(angle)
    sine = jnp.sin(angle)
    return (jnp.concatenate([cosine, cosine], 1), jnp.concatenate([sine, sine], 1))

def rotate(vector, cosine, sine):
    half = vector.shape[-1] // 2
    turned = jnp.concatenate([-vector[..., half:], vector[..., :half]], -1)
    return vector * cosine + turned * sine

def unrotate(grad, cosine, sine):
    half = grad.shape[-1] // 2
    turned = jnp.concatenate([grad[..., half:], -grad[..., :half]], -1)
    return grad * cosine + turned * sine

def attend_back(query, key, value, cot, keep, cosine, sine, scale):
    batch, seq, heads_q, dim = query.shape
    heads_k = key.shape[2]
    group = heads_q // heads_k
    grouped = query.reshape(batch, seq, heads_k, group, dim).astype(jnp.float32)
    cot_grouped = cot.reshape(batch, seq, heads_k, group, dim).astype(jnp.float32)
    complete_keys = key.astype(jnp.float32)
    complete_values = value.astype(jnp.float32)
    raw = jnp.einsum('bqkgd,bskd->bkgqs', grouped, complete_keys) * scale
    bend = jnp.tanh(raw / cap_value)
    weights = jnp.where(keep[:, None, None], jnp.exp(cap_value * bend), 0.0)
    probs = weights / lax.optimization_barrier(jnp.sum(weights, -1, keepdims=True))
    probs_b = rounded(probs)
    noisy_value_gradient = jnp.einsum('bkgqs,bqkgd->bskd', probs_b, cot_grouped).astype(jnp.bfloat16)
    grad_probs = jnp.einsum('bqkgd,bskd->bkgqs', cot_grouped, complete_values)
    delta = lax.optimization_barrier(jnp.sum(probs * grad_probs, -1, keepdims=True))
    grad_scores = rounded(probs * (grad_probs - delta) * (1.0 - bend * bend) * scale)
    noisy_key_gradient = jnp.einsum('bkgqs,bqkgd->bskd', grad_scores, grouped)
    noisy_key_gradient = unrotate(noisy_key_gradient, cosine[:, None, :], sine[:, None, :]).astype(jnp.bfloat16)
    return (noisy_key_gradient.reshape(batch, seq, heads_k * dim), noisy_value_gradient.reshape(batch, seq, heads_k * dim))

def group_terms(x_rows, cot_rows, group_lengths, group_sampled, w_query, w_key, w_value, cosine, sine):
    seq_dev = group_lengths.shape[0]
    length = x_rows.shape[0] // seq_dev
    scale = float(D // H) ** (-0.5)
    query = jnp.dot(x_rows, w_query, preferred_element_type=jnp.float32).reshape(seq_dev, length, H, HD)
    key = jnp.dot(x_rows, w_key, preferred_element_type=jnp.float32).reshape(seq_dev, length, KV, HD)
    value = jnp.dot(x_rows, w_value, preferred_element_type=jnp.float32).reshape(seq_dev, length, KV, HD)
    query = rotate(query, cosine[:, None, :], sine[:, None, :]).astype(jnp.bfloat16)
    key = rotate(key, cosine[:, None, :], sine[:, None, :]).astype(jnp.bfloat16)
    value = value.astype(jnp.bfloat16)
    position = jnp.arange(length, dtype=jnp.int32)
    valid = (position[None, :] < group_lengths[:, None]) & (group_sampled[:, None] > 0)
    cot = jnp.where(valid[:, :, None], cot_rows.reshape(seq_dev, length, H * HD), jnp.zeros((), jnp.bfloat16))
    cot = cot.astype(jnp.bfloat16).reshape(seq_dev, length, H, HD)
    keep = (position[:, None] >= position[None, :])[None] & (position[None, None, :] < group_lengths[:, None, None])
    noisy_key_gradient, noisy_value_gradient = attend_back(query, key, value, cot, keep, cosine, sine, scale)
    sequence_batch = x_rows.reshape(seq_dev, length, D).astype(jnp.float32)
    input_inner_products = jnp.einsum('gwv,gtv->gwt', sequence_batch, sequence_batch)
    complete_keys = noisy_key_gradient.astype(jnp.float32)
    complete_values = noisy_value_gradient.astype(jnp.float32)
    key_inner_products = jnp.einsum('gwv,gtv->gwt', complete_keys, complete_keys)
    value_inner_products = jnp.einsum('gwv,gtv->gwt', complete_values, complete_values)
    norm_key = jnp.sqrt(lax.optimization_barrier(jnp.sum(input_inner_products * key_inner_products, (1, 2))))
    norm_value = jnp.sqrt(lax.optimization_barrier(jnp.sum(input_inner_products * value_inner_products, (1, 2))))
    clip_bound = 2.0 * math.sqrt(D * KV * HD)
    factor_key = clip_bound / jnp.maximum(norm_key, clip_bound)
    factor_value = clip_bound / jnp.maximum(norm_value, clip_bound)
    scaled_key = (factor_key[:, None, None] * complete_keys).astype(jnp.bfloat16).reshape(seq_dev * length, KV * HD)
    scaled_value = (factor_value[:, None, None] * complete_values).astype(jnp.bfloat16).reshape(seq_dev * length, KV * HD)
    term_key = jnp.dot(x_rows.T, scaled_key, preferred_element_type=jnp.float32)
    term_value = jnp.dot(x_rows.T, scaled_value, preferred_element_type=jnp.float32)
    return (term_key, term_value)

def reference(inputs, w_query, w_key, w_value, cotangent, lengths, sampled, step, tree_noise):
    cosine, sine = rope_tables(L, HD)
    x_groups = inputs.reshape(N_DP, SEQ_DEV * L, D)
    cot_groups = cotangent.reshape(N_DP, SEQ_DEV * L, H * HD)
    length_groups = lengths.reshape(N_DP, SEQ_DEV)
    sampled_groups = sampled.reshape(N_DP, SEQ_DEV)

    def one_group(carry, pieces):
        term_key, term_value = group_terms(pieces[0], pieces[1], pieces[2], pieces[3], w_query, w_key, w_value, cosine, sine)
        return ((carry[0] + rounded(term_key), carry[1] + rounded(term_value)), None)
    start = (jnp.zeros((D, KV * HD), jnp.float32), jnp.zeros((D, KV * HD), jnp.float32))
    sums, unused = lax.scan(one_group, start, (x_groups, cot_groups, length_groups, sampled_groups))
    bits = (step[0] // 2 ** jnp.arange(LEVELS, dtype=jnp.int32) % 2).astype(jnp.float32)
    noise = lax.optimization_barrier(jnp.sum(bits[:, None, None, None] * tree_noise, 0))
    expected = 0.85 * SEQS
    return (sums[0] / expected + noise[0], sums[1] / expected + noise[1])
```

```python
import functools
import math

import jax
import jax.numpy as jnp
import numpy as np
from jax import lax
from jax.experimental import pallas as pl
from jax.experimental.pallas import tpu as pltpu
from jax.sharding import Mesh
from jax.sharding import PartitionSpec as P

D = 4608
H = 32
KV = 16
HD = 128
L = 256
NZ, NX, NY, NC = 8, 4, 8, 2
SHARD = D // (NY * NC)
PAIR = NC * SHARD
TOKENS = 2 * L
CAP = 50.0
SCALE = float(D // H) ** (-0.5)
CLIP = 2.0 * math.sqrt(D * KV * HD)
VMEM = 48 * 1024 * 1024
F32 = jnp.float32
BF16 = jnp.bfloat16

NN = (((1,), (0,)), ((), ()))
NT = (((1,), (1,)), ((), ()))


def dot(a, b, dims=NN):
    return lax.dot_general(a, b, dims, preferred_element_type=F32)


def ring(n, k):
    return [((i + k) % n, i) for i in range(n)]


def rope_tables(length, dim):
    half = dim // 2
    freq = 10000.0 ** (-(jnp.arange(half, dtype=F32) * (2.0 / dim)))
    angle = jnp.arange(length, dtype=F32)[:, None] * freq[None, :]
    cosine = jnp.cos(angle)
    sine = jnp.sin(angle)
    return jnp.concatenate([cosine, cosine], 1), jnp.concatenate([-sine, sine], 1)


def arrange_kernel(place, mine, other, x_t, x_tok, gram):
    k = pl.program_id(0)
    first = place[1] == 0
    a = mine[0]
    b = other[0]
    block = jnp.concatenate([jnp.where(first, a, b), jnp.where(first, b, a)], 0)
    x_t[...] = block
    rows = block.T
    x_tok[0] = rows

    @pl.when(k == 0)
    def _():
        gram[...] = jnp.zeros_like(gram)

    for s in range(2):
        part = rows[s * L : (s + 1) * L]
        gram[s] += dot(part, part, NT)


def arrange(place, mine, other):
    return pl.pallas_call(
        arrange_kernel,
        grid_spec=pltpu.PrefetchScalarGridSpec(
            num_scalar_prefetch=1,
            grid=(NY,),
            in_specs=[
                pl.BlockSpec((1, SHARD, TOKENS), lambda k, p: (k, 0, 0)),
                pl.BlockSpec((1, SHARD, TOKENS), lambda k, p: (k, 0, 0)),
            ],
            out_specs=[
                pl.BlockSpec((PAIR, TOKENS), lambda k, p: ((p[0] + k) % NY, 0)),
                pl.BlockSpec((1, TOKENS, PAIR), lambda k, p: ((p[0] + k) % NY, 0, 0)),
                pl.BlockSpec((2, L, L), lambda k, p: (0, 0, 0)),
            ],
        ),
        out_shape=[
            jax.ShapeDtypeStruct((D, TOKENS), BF16),
            jax.ShapeDtypeStruct((NY, TOKENS, PAIR), BF16),
            jax.ShapeDtypeStruct((2, L, L), F32),
        ],
        compiler_params=pltpu.CompilerParams(vmem_limit_bytes=VMEM),
        cost_estimate=pl.CostEstimate(
            flops=2 * 2 * L * L * D, bytes_accessed=3 * 2 * D * TOKENS, transcendentals=0
        ),
        name="arrange",
    )(place, mine, other)


def attend_kernel(info, x_tok, w, cot, cosine, sine, gram, dk_out, dv_out, norms, acc):
    k = pl.program_id(0)
    part = dot(x_tok[0], w[...])

    @pl.when(k == 0)
    def _():
        acc[...] = part

    @pl.when(k > 0)
    def _():
        acc[...] += part

    @pl.when(k == NY - 1)
    def _():
        cos = cosine[...]
        sin = sine[...]
        key_at = lax.broadcasted_iota(jnp.int32, (L, L), 0)
        query_at = lax.broadcasted_iota(jnp.int32, (L, L), 1)
        row_at = lax.broadcasted_iota(jnp.int32, (L, HD), 0)

        def rotated(u):
            return (u * cos + pltpu.roll(u, HD // 2, 1) * sin).astype(BF16)

        for s in range(2):
            rows = slice(s * L, (s + 1) * L)
            length = info[s]
            valid = (row_at < length) & (info[2 + s] > 0)
            keep = (key_at <= query_at) & (key_at < length)
            key = rotated(acc[rows, 2 * HD : 3 * HD])
            value = acc[rows, 3 * HD : 4 * HD].astype(BF16)
            dv = jnp.zeros((L, HD), F32)
            dk_rot = jnp.zeros((L, HD), F32)
            for j in range(2):
                query = rotated(acc[rows, j * HD : (j + 1) * HD])
                grad = jnp.where(valid, cot[rows, j * HD : (j + 1) * HD], jnp.zeros((), BF16))
                bend = jnp.tanh(dot(key, query, NT) * (SCALE / CAP))
                weights = jnp.where(keep, jnp.exp(CAP * bend), 0.0)
                probs = weights * (1.0 / jnp.sum(weights, 0, keepdims=True))
                dv += dot(probs.astype(BF16), grad)
                grad_probs = dot(value, grad, NT)
                delta = jnp.sum(probs * grad_probs, 0, keepdims=True)
                ds = probs * (grad_probs - delta) * ((1.0 - bend * bend) * SCALE)
                dk_rot += dot(ds.astype(BF16), query)
            dk = (dk_rot * cos - pltpu.roll(dk_rot, HD // 2, 1) * sin).astype(BF16)
            dv = dv.astype(BF16)
            dk_out[rows] = dk
            dv_out[rows] = dv
            for i, d in enumerate((dk, dv)):
                folded = jnp.sum(gram[s] * dot(d, d, NT), 0, keepdims=True)
                norms[2 * i + s : 2 * i + s + 1] = folded[:, :HD] + folded[:, HD:]


def attend(info, x_tok, w, cot, cosine, sine, gram):
    whole = lambda *shape: pl.BlockSpec(shape, lambda k, p: (0,) * len(shape))
    return pl.pallas_call(
        attend_kernel,
        grid_spec=pltpu.PrefetchScalarGridSpec(
            num_scalar_prefetch=1,
            grid=(NY,),
            in_specs=[
                pl.BlockSpec((1, TOKENS, PAIR), lambda k, p: (k, 0, 0)),
                pl.BlockSpec((PAIR, 4 * HD), lambda k, p: (k, 0)),
                whole(TOKENS, 2 * HD),
                whole(L, HD),
                whole(L, HD),
                whole(2, L, L),
            ],
            out_specs=[whole(TOKENS, HD), whole(TOKENS, HD), whole(4, HD)],
            scratch_shapes=[pltpu.VMEM((TOKENS, 4 * HD), F32)],
        ),
        out_shape=[
            jax.ShapeDtypeStruct((TOKENS, HD), BF16),
            jax.ShapeDtypeStruct((TOKENS, HD), BF16),
            jax.ShapeDtypeStruct((4, HD), F32),
        ],
        compiler_params=pltpu.CompilerParams(vmem_limit_bytes=VMEM),
        cost_estimate=pl.CostEstimate(
            flops=2 * TOKENS * 4 * HD * D + 4 * 12 * L * L * HD,
            bytes_accessed=4 * D * TOKENS,
            transcendentals=8 * L * L,
        ),
        name="attend",
    )(info, x_tok, w, cot, cosine, sine, gram)


def gradient_kernel(x_t, dk, dv, norms, out, scaled):
    @pl.when(pl.program_id(0) == 0)
    def _():
        for i, d in enumerate((dk, dv)):
            for s in range(2):
                total = jnp.sum(norms[:, 2 * i + s, :])
                factor = CLIP / jnp.maximum(jnp.sqrt(jnp.broadcast_to(total, (1, HD))), CLIP)
                rows = slice(s * L, (s + 1) * L)
                scaled[rows, i * HD : (i + 1) * HD] = (factor * d[rows].astype(F32)).astype(BF16)

    out[...] = dot(x_t[...], scaled[...]).astype(BF16)


def gradient(x_t, dk, dv, norms):
    whole = lambda *shape: pl.BlockSpec(shape, lambda k: (0,) * len(shape))
    return pl.pallas_call(
        gradient_kernel,
        grid=(NY,),
        in_specs=[
            pl.BlockSpec((PAIR, TOKENS), lambda k: (k, 0)),
            whole(TOKENS, HD),
            whole(TOKENS, HD),
            whole(NY, 4, HD),
        ],
        out_specs=pl.BlockSpec((PAIR, 2 * HD), lambda k: (k, 0)),
        out_shape=jax.ShapeDtypeStruct((D, 2 * HD), BF16),
        scratch_shapes=[pltpu.VMEM((TOKENS, 2 * HD), BF16)],
        compiler_params=pltpu.CompilerParams(vmem_limit_bytes=VMEM),
        cost_estimate=pl.CostEstimate(
            flops=2 * D * TOKENS * 2 * HD, bytes_accessed=3 * D * TOKENS, transcendentals=0
        ),
        name="gradient",
    )(x_t, dk, dv, norms)


def body(inputs, w_query, w_key, w_value, cotangent, lengths, sampled, step, tree_noise):
    w = jnp.concatenate([w_query, w_key, w_value], 1)
    w = lax.all_gather(w, "x", axis=0, tiled=True)
    w, shard = lax.optimization_barrier((w, inputs.T))
    w = lax.all_gather(w, "z", axis=0, tiled=True)

    mine = jnp.stack([shard] + [lax.ppermute(shard, "y", ring(NY, k)) for k in range(1, NY)])
    other = lax.ppermute(mine, "core", ring(NC, 1))
    place = jnp.stack([lax.axis_index("y"), lax.axis_index("core")]).astype(jnp.int32)
    x_t, x_tok, gram = arrange(place, mine, other)

    cosine, sine = rope_tables(L, HD)
    dk, dv, norms = attend(
        jnp.concatenate([lengths, sampled]), x_tok, w, cotangent, cosine, sine, gram
    )
    norms = lax.psum(norms, "core")
    norms = lax.all_to_all(jnp.broadcast_to(norms, (NY, 4, HD)), "y", 0, 0)
    terms = gradient(x_t, dk, dv, norms)
    terms = lax.all_to_all(terms.reshape(NZ * NX, D // (NZ * NX), 2 * HD), ("z", "x"), 0, 0)
    summed = jnp.sum(terms.astype(F32), 0)

    levels = tree_noise.shape[0]
    bits = (step[0] // 2 ** jnp.arange(levels, dtype=jnp.int32) % 2).astype(F32)
    noise = jnp.sum(bits[:, None, None, None] * tree_noise, 0)
    expected = 0.85 * (2 * NZ * NX)
    return summed[:, :HD] / expected + noise[0], summed[:, HD:] / expected + noise[1]


def solution(mesh):
    mesh = Mesh(np.asarray(mesh.devices).reshape(NZ, NX, NY, NC), ("z", "x", "y", "core"))
    dp, head = ("z", "x"), ("y", "core")
    in_specs = (
        P(dp, head),
        P(dp, head),
        P(dp, head),
        P(dp, head),
        P(dp, head),
        P(dp),
        P(dp),
        P(),
        P(None, None, dp, head),
    )
    out_specs = (P(dp, head), P(dp, head))
    return jax.shard_map(body, mesh=mesh, in_specs=in_specs, out_specs=out_specs, check_vma=False)
```

```python
import functools
import math

import jax
import jax.numpy as jnp
import numpy as np
from jax import lax
from jax.experimental import pallas as pl
from jax.experimental.pallas import tpu as pltpu
from jax.sharding import Mesh
from jax.sharding import PartitionSpec as P

D = 4608
H = 32
KV = 16
HD = 128
L = 256
NZ, NX, NY, NC = 8, 4, 8, 2
SHARD = D // (NY * NC)
PAIR = NC * SHARD
ROWS = D // (NZ * NX)
TOKENS = 2 * L
CAP = 50.0
SCALE = float(D // H) ** (-0.5)
CLIP = 2.0 * math.sqrt(D * KV * HD)
CHUNK = 2 * PAIR
FETCH = 768
VMEM = 32 * 1024 * 1024
VMEM_MOST = 54 * 1024 * 1024
F32 = jnp.float32
BF16 = jnp.bfloat16

NN = (((1,), (0,)), ((), ()))
NT = (((1,), (1,)), ((), ()))


def dot(a, b, dims=NN):
    return lax.dot_general(a, b, dims, preferred_element_type=F32)


def ring(n, k):
    return [((i + k) % n, i) for i in range(n)]


def rope_tables(length, dim):
    half = dim // 2
    freq = 10000.0 ** (-(jnp.arange(half, dtype=F32) * (2.0 / dim)))
    angle = jnp.arange(length, dtype=F32)[:, None] * freq[None, :]
    cosine = jnp.cos(angle)
    sine = jnp.sin(angle)
    return jnp.concatenate([cosine, cosine], 1), jnp.concatenate([-sine, sine], 1)


def arrange_kernel(place, mine, other, x_tok, gram, held, sems):
    first = place[1] == 0
    for m in range(NY // 2):
        columns = slice(m * CHUNK, (m + 1) * CHUNK)
        parts = []
        for half in range(2):
            at = lax.rem(2 * m + half + NY - place[0], NY)
            a = mine[at]
            b = other[at]
            parts += [jnp.where(first, a, b), jnp.where(first, b, a)]
        rows = jnp.concatenate(parts, 0).T
        held[:, columns] = rows
        pltpu.make_async_copy(held.at[:, columns], x_tok.at[:, columns], sems.at[m]).start()
        for s in range(2):
            part = rows[s * L : (s + 1) * L]
            product = dot(part, part, NT)
            gram[s] = product if m == 0 else gram[s] + product
    for m in range(NY // 2):
        columns = slice(m * CHUNK, (m + 1) * CHUNK)
        pltpu.make_async_copy(held.at[:, columns], x_tok.at[:, columns], sems.at[m]).wait()


def arrange(place, mine, other):
    vmem = pl.BlockSpec(memory_space=pltpu.VMEM)
    return pl.pallas_call(
        arrange_kernel,
        in_specs=[pl.BlockSpec(memory_space=pltpu.SMEM), vmem, vmem],
        out_specs=[pl.BlockSpec(memory_space=pl.ANY), vmem],
        out_shape=[
            jax.ShapeDtypeStruct((TOKENS, D), BF16),
            jax.ShapeDtypeStruct((2, L, L), F32),
        ],
        scratch_shapes=[
            pltpu.VMEM((TOKENS, D), BF16),
            pltpu.SemaphoreType.DMA((NY // 2,)),
        ],
        compiler_params=pltpu.CompilerParams(vmem_limit_bytes=VMEM_MOST),
        cost_estimate=pl.CostEstimate(
            flops=2 * 2 * L * L * D, bytes_accessed=2 * 2 * D * TOKENS, transcendentals=0
        ),
        name="arrange",
    )(place, mine, other)


def attend_kernel(
    info, x_tok, w, cot, cosine, sine, gram, grads, norms, x_held, w_held, acc, sems
):
    def fetch(m):
        part = pl.ds(m * FETCH, FETCH)
        return (
            pltpu.make_async_copy(x_tok.at[:, part], x_held.at[:, part], sems.at[0, m]),
            pltpu.make_async_copy(w.at[part], w_held.at[part], sems.at[1, m]),
        )

    for m in range(D // FETCH):
        for copy in fetch(m):
            copy.start()
    acc[...] = jnp.zeros_like(acc)

    for m in range(D // FETCH):
        for copy in fetch(m):
            copy.wait()
        part = pl.ds(m * FETCH, FETCH)
        acc[...] += dot(x_held[:, part], w_held[part])

    cos = cosine[...]
    sin = sine[...]
    key_at = lax.broadcasted_iota(jnp.int32, (L, L), 0)
    query_at = lax.broadcasted_iota(jnp.int32, (L, L), 1)
    row_at = lax.broadcasted_iota(jnp.int32, (L, HD), 0)

    def rotated(u):
        return (u * cos + pltpu.roll(u, HD // 2, 1) * sin).astype(BF16)

    for s in range(2):
        rows = slice(s * L, (s + 1) * L)
        length = info[s]
        valid = (row_at < length) & (info[2 + s] > 0)
        keep = (key_at <= query_at) & (key_at < length)
        key = rotated(acc[rows, 2 * HD : 3 * HD])
        value = acc[rows, 3 * HD : 4 * HD].astype(BF16)
        dv = jnp.zeros((L, HD), F32)
        dk_rot = jnp.zeros((L, HD), F32)
        for j in range(2):
            query = rotated(acc[rows, j * HD : (j + 1) * HD])
            grad = jnp.where(valid, cot[rows, j * HD : (j + 1) * HD], jnp.zeros((), BF16))
            bend = jnp.tanh(dot(key, query, NT) * (SCALE / CAP))
            weights = jnp.where(keep, jnp.exp(CAP * bend), 0.0)
            probs = weights * (1.0 / jnp.sum(weights, 0, keepdims=True))
            dv += dot(probs.astype(BF16), grad)
            grad_probs = dot(value, grad, NT)
            delta = jnp.sum(probs * grad_probs, 0, keepdims=True)
            ds = probs * (grad_probs - delta) * ((1.0 - bend * bend) * SCALE)
            dk_rot += dot(ds.astype(BF16), query)
        dk = (dk_rot * cos - pltpu.roll(dk_rot, HD // 2, 1) * sin).astype(BF16)
        dv = dv.astype(BF16)
        for i, d in enumerate((dk, dv)):
            grads[rows, i * HD : (i + 1) * HD] = d
            folded = jnp.sum(gram[s] * dot(d, d, NT), 0, keepdims=True)
            norms[2 * i + s : 2 * i + s + 1] = folded[:, :HD] + folded[:, HD:]


def attend(info, x_tok, w, cot, cosine, sine, gram):
    vmem = pl.BlockSpec(memory_space=pltpu.VMEM)
    return pl.pallas_call(
        attend_kernel,
        in_specs=[pl.BlockSpec(memory_space=pltpu.SMEM)]
        + [pl.BlockSpec(memory_space=pl.ANY)] * 2
        + [vmem] * 4,
        out_specs=[vmem] * 2,
        out_shape=[
            jax.ShapeDtypeStruct((TOKENS, 2 * HD), BF16),
            jax.ShapeDtypeStruct((4, HD), F32),
        ],
        scratch_shapes=[
            pltpu.VMEM((TOKENS, D), BF16),
            pltpu.VMEM((D, 4 * HD), BF16),
            pltpu.VMEM((TOKENS, 4 * HD), F32),
            pltpu.SemaphoreType.DMA((2, D // FETCH)),
        ],
        compiler_params=pltpu.CompilerParams(vmem_limit_bytes=VMEM_MOST),
        cost_estimate=pl.CostEstimate(
            flops=2 * TOKENS * 4 * HD * D + 4 * 12 * L * L * HD,
            bytes_accessed=4 * D * TOKENS,
            transcendentals=8 * L * L,
        ),
        name="attend",
    )(info, x_tok, w, cot, cosine, sine, gram)


def gradient_kernel(place, mine, other, grads, norms, out, scaled):
    for i in range(2):
        for s in range(2):
            total = jnp.sum(norms[:, 2 * i + s, :])
            factor = CLIP / jnp.maximum(jnp.sqrt(jnp.broadcast_to(total, (1, HD))), CLIP)
            rows = slice(s * L, (s + 1) * L)
            columns = slice(i * HD, (i + 1) * HD)
            scaled[rows, columns] = (factor * grads[rows, columns].astype(F32)).astype(BF16)

    @pl.loop(0, NY, unroll=NY)
    def _(k):
        at = lax.rem(place[0] + k, NY)
        for held, core in ((mine, place[1]), (other, 1 - place[1])):
            part = dot(held[k], scaled[...]).astype(BF16)
            out[2 * core, at] = part[:ROWS]
            out[2 * core + 1, at] = part[ROWS:]


def gradient(place, mine, other, grads, norms):
    vmem = pl.BlockSpec(memory_space=pltpu.VMEM)
    return pl.pallas_call(
        gradient_kernel,
        in_specs=[pl.BlockSpec(memory_space=pltpu.SMEM)] + [vmem] * 4,
        out_specs=vmem,
        out_shape=jax.ShapeDtypeStruct((NX, NZ, ROWS, 2 * HD), BF16),
        scratch_shapes=[pltpu.VMEM((TOKENS, 2 * HD), BF16)],
        compiler_params=pltpu.CompilerParams(vmem_limit_bytes=VMEM),
        cost_estimate=pl.CostEstimate(
            flops=2 * D * TOKENS * 2 * HD, bytes_accessed=3 * D * TOKENS, transcendentals=0
        ),
        name="gradient",
    )(place, mine, other, grads, norms)


def gather_y(shard):
    hop = lambda a, k: lax.ppermute(a, "y", ring(NY, k))
    up, down = [shard], [shard]
    for _ in range(3):
        up.append(hop(up[-1], 1))
        down.append(hop(down[-1], 7))
    return jnp.stack(up + [hop(up[-1], 1)] + down[:0:-1])


def reduce_rows(terms):
    terms = lax.all_to_all(terms, "x", 0, 0)
    terms = jnp.sum(terms.astype(F32), 0).astype(BF16)
    terms = lax.all_to_all(terms, "z", 0, 0)
    return jnp.sum(terms.astype(F32), 0)


def body(inputs, w_query, w_key, w_value, cotangent, lengths, sampled, step, tree_noise):
    w = jnp.concatenate([w_query, w_key, w_value], 1)
    w = lax.all_gather(w, "x", axis=0, tiled=True)
    w, shard = lax.optimization_barrier((w, inputs.T))
    w = lax.all_gather(w, "z", axis=0, tiled=True)

    mine = gather_y(shard)
    other = lax.ppermute(mine, "core", ring(NC, 1))
    place = jnp.stack([lax.axis_index("y"), lax.axis_index("core")]).astype(jnp.int32)
    x_tok, gram = arrange(place, mine, other)

    cosine, sine = rope_tables(L, HD)
    grads, norms = attend(
        jnp.concatenate([lengths, sampled]), x_tok, w, cotangent, cosine, sine, gram
    )
    norms = lax.psum(norms, "core")
    norms = lax.all_to_all(jnp.broadcast_to(norms, (NY, 4, HD)), "y", 0, 0)
    terms = gradient(place, mine, other, grads, norms)
    summed = reduce_rows(terms)

    levels = tree_noise.shape[0]
    bits = (step[0] // 2 ** jnp.arange(levels, dtype=jnp.int32) % 2).astype(F32)
    noise = jnp.sum(bits[:, None, None, None] * tree_noise, 0)
    expected = 0.85 * (2 * NZ * NX)
    return summed[:, :HD] / expected + noise[0], summed[:, HD:] / expected + noise[1]


def solution(mesh):
    mesh = Mesh(np.asarray(mesh.devices).reshape(NZ, NX, NY, NC), ("z", "x", "y", "core"))
    dp, head = ("z", "x"), ("y", "core")
    in_specs = (
        P(dp, head),
        P(dp, head),
        P(dp, head),
        P(dp, head),
        P(dp, head),
        P(dp),
        P(dp),
        P(),
        P(None, None, dp, head),
    )
    out_specs = (P(dp, head), P(dp, head))
    return jax.shard_map(body, mesh=mesh, in_specs=in_specs, out_specs=out_specs, check_vma=False)
```

```python
import functools
import math

import jax
import jax.numpy as jnp
import numpy as np
from jax import lax
from jax.experimental import pallas as pl
from jax.experimental.pallas import tpu as pltpu
from jax.sharding import Mesh
from jax.sharding import PartitionSpec as P

D = 4608
H = 32
KV = 16
HD = 128
L = 256
NZ, NX, NY, NC = 8, 4, 8, 2
SHARD = D // (NY * NC)
PAIR = NC * SHARD
ROWS = D // (NZ * NX)
TOKENS = 2 * L
CAP = 50.0
SCALE = float(D // H) ** (-0.5)
CLIP = 2.0 * math.sqrt(D * KV * HD)
CHUNK = 2 * PAIR
VMEM = 32 * 1024 * 1024
VMEM_ATTEND = 52 * 1024 * 1024
VMEM_MOST = 58 * 1024 * 1024
F32 = jnp.float32
BF16 = jnp.bfloat16

NN = (((1,), (0,)), ((), ()))
NT = (((1,), (1,)), ((), ()))


def dot(a, b, dims=NN):
    return lax.dot_general(a, b, dims, preferred_element_type=F32)


def ring(n, k):
    return [((i + k) % n, i) for i in range(n)]


def rope_tables(length, dim):
    half = dim // 2
    freq = 10000.0 ** (-(jnp.arange(half, dtype=F32) * (2.0 / dim)))
    angle = jnp.arange(length, dtype=F32)[:, None] * freq[None, :]
    cosine = jnp.cos(angle)
    sine = jnp.sin(angle)
    return jnp.concatenate([cosine, cosine], 1), jnp.concatenate([-sine, sine], 1)


def gram_kernel(place, mine, other, gram, own):
    x = place[2]
    half = pl.ds(pl.multiple_of(lax.rem(x, 2) * ROWS, ROWS), ROWS)
    here = x // 2 == place[1]
    for m in range(NY // 2):
        for k in (2 * m, 2 * m + 1):
            own[lax.rem(place[0] + k, NY)] = jnp.where(here, mine[k, half], other[k, half])
        parts = [mine[2 * m], other[2 * m], mine[2 * m + 1], other[2 * m + 1]]
        rows = jnp.concatenate(parts, 0).T
        for s in range(2):
            part = rows[s * L : (s + 1) * L]
            product = dot(part, part, NT)
            gram[s] = product if m == 0 else gram[s] + product


def gram_of(place, mine, other):
    vmem = pl.BlockSpec(memory_space=pltpu.VMEM)
    return pl.pallas_call(
        gram_kernel,
        in_specs=[pl.BlockSpec(memory_space=pltpu.SMEM)] + [vmem] * 2,
        out_specs=[vmem] * 2,
        out_shape=[
            jax.ShapeDtypeStruct((2, L, L), F32),
            jax.ShapeDtypeStruct((NZ, ROWS, TOKENS), BF16),
        ],
        compiler_params=pltpu.CompilerParams(vmem_limit_bytes=VMEM),
        cost_estimate=pl.CostEstimate(
            flops=2 * 2 * L * L * D, bytes_accessed=2 * D * TOKENS, transcendentals=0
        ),
        name="gram",
    )(place, mine, other)


def attend_kernel(
    info, place, mine, other, w, cot, cosine, sine, gram, grads, norms, x_tok, held, acc, sems
):
    def fetch(m):
        part = pl.ds(m * CHUNK, CHUNK)
        return pltpu.make_async_copy(w.at[part], held.at[part], sems.at[m])

    for m in range(NY // 2):
        fetch(m).start()
    first = place[1] == 0
    for m in range(NY // 2):
        parts = []
        for half in range(2):
            at = lax.rem(2 * m + half + NY - place[0], NY)
            a, b = mine[at], other[at]
            parts += [jnp.where(first, a, b), jnp.where(first, b, a)]
        x_tok[:, m * CHUNK : (m + 1) * CHUNK] = jnp.concatenate(parts, 0).T
    for m in range(NY // 2):
        fetch(m).wait()
        part = slice(m * CHUNK, (m + 1) * CHUNK)
        product = dot(x_tok[:, part], held[part])
        acc[...] = product if m == 0 else acc[...] + product

    cos = cosine[...]
    sin = sine[...]
    key_at = lax.broadcasted_iota(jnp.int32, (L, L), 0)
    query_at = lax.broadcasted_iota(jnp.int32, (L, L), 1)
    row_at = lax.broadcasted_iota(jnp.int32, (L, HD), 0)

    def rotated(u):
        return (u * cos + pltpu.roll(u, HD // 2, 1) * sin).astype(BF16)

    for s in range(2):
        rows = slice(s * L, (s + 1) * L)
        length = info[s]
        valid = (row_at < length) & (info[2 + s] > 0)
        keep = (key_at <= query_at) & (key_at < length)
        key = rotated(acc[rows, 2 * HD : 3 * HD])
        value = acc[rows, 3 * HD : 4 * HD].astype(BF16)
        dv = jnp.zeros((L, HD), F32)
        dk_rot = jnp.zeros((L, HD), F32)
        for j in range(2):
            query = rotated(acc[rows, j * HD : (j + 1) * HD])
            grad = jnp.where(valid, cot[rows, j * HD : (j + 1) * HD], jnp.zeros((), BF16))
            bend = jnp.tanh(dot(key, query, NT) * (SCALE / CAP))
            weights = jnp.where(keep, jnp.exp(CAP * bend), 0.0)
            probs = weights * (1.0 / jnp.sum(weights, 0, keepdims=True))
            dv += dot(probs.astype(BF16), grad)
            grad_probs = dot(value, grad, NT)
            delta = jnp.sum(probs * grad_probs, 0, keepdims=True)
            ds = probs * (grad_probs - delta) * ((1.0 - bend * bend) * SCALE)
            dk_rot += dot(ds.astype(BF16), query)
        dk = (dk_rot * cos - pltpu.roll(dk_rot, HD // 2, 1) * sin).astype(BF16)
        dv = dv.astype(BF16)
        for i, d in enumerate((dk, dv)):
            grads[rows, i * HD : (i + 1) * HD] = d
            folded = jnp.sum(gram[s] * dot(d, d, NT), 0, keepdims=True)
            norms[2 * i + s : 2 * i + s + 1] = folded[:, :HD] + folded[:, HD:]


def attend(info, place, mine, other, w, cot, cosine, sine, gram):
    smem = pl.BlockSpec(memory_space=pltpu.SMEM)
    vmem = pl.BlockSpec(memory_space=pltpu.VMEM)
    return pl.pallas_call(
        attend_kernel,
        in_specs=[smem] * 2 + [vmem] * 2 + [pl.BlockSpec(memory_space=pl.ANY)] + [vmem] * 4,
        out_specs=[vmem] * 2,
        out_shape=[
            jax.ShapeDtypeStruct((TOKENS, 2 * HD), BF16),
            jax.ShapeDtypeStruct((4, HD), F32),
        ],
        scratch_shapes=[
            pltpu.VMEM((TOKENS, D), BF16),
            pltpu.VMEM((D, 4 * HD), BF16),
            pltpu.VMEM((TOKENS, 4 * HD), F32),
            pltpu.SemaphoreType.DMA((NY // 2,)),
        ],
        compiler_params=pltpu.CompilerParams(vmem_limit_bytes=VMEM_ATTEND),
        cost_estimate=pl.CostEstimate(
            flops=2 * TOKENS * 4 * HD * D + 4 * 12 * L * L * HD,
            bytes_accessed=4 * D * TOKENS,
            transcendentals=8 * L * L,
        ),
        name="attend",
    )(info, place, mine, other, w, cot, cosine, sine, gram)


def clip_kernel(place, norms, *refs):
    grads, scaled = refs[:NX], refs[NX]
    for j in range(NX):
        x = lax.rem(place[2] + j, NX)
        sums = jnp.sum(jnp.sum(norms[x], 0), 1, keepdims=True)
        factors = CLIP / jnp.maximum(jnp.sqrt(sums), CLIP)
        for s in range(2):
            rows = slice(s * L, (s + 1) * L)
            for i in range(2):
                columns = slice(i * HD, (i + 1) * HD)
                factor = factors[2 * i + s : 2 * i + s + 1, :]
                part = factor * grads[j][rows, columns].astype(F32)
                scaled[j * TOKENS + s * L : j * TOKENS + (s + 1) * L, columns] = part.astype(BF16)


def clip(place, norms, grads):
    vmem = pl.BlockSpec(memory_space=pltpu.VMEM)
    return pl.pallas_call(
        clip_kernel,
        in_specs=[pl.BlockSpec(memory_space=pltpu.SMEM)] + [vmem] * (NX + 1),
        out_specs=vmem,
        out_shape=jax.ShapeDtypeStruct((NX * TOKENS, 2 * HD), BF16),
        compiler_params=pltpu.CompilerParams(vmem_limit_bytes=VMEM),
        name="clip",
    )(place, norms, *grads)


def gradient_kernel(features, own, scaled, out, held, sems):
    def fetch(j, s):
        columns = pl.ds((2 * (j - 1) + s) * L, L)
        return pltpu.make_async_copy(
            features.at[:, s, j - 1], held.at[:, :, columns], sems.at[2 * (j - 1) + s]
        )

    for j in range(1, NX):
        for s in range(2):
            fetch(j, s).start()
    total = dot(own[...].reshape(NZ * ROWS, TOKENS), scaled[:TOKENS])
    for j in range(1, NX):
        for s in range(2):
            fetch(j, s).wait()
        rows = held[:, :, (j - 1) * TOKENS : j * TOKENS].reshape(NZ * ROWS, TOKENS)
        total += dot(rows, scaled[j * TOKENS : (j + 1) * TOKENS])
    out[...] = total.astype(BF16).reshape(NZ, ROWS, 2 * HD)


def gradient(features, own, scaled):
    vmem = pl.BlockSpec(memory_space=pltpu.VMEM)
    return pl.pallas_call(
        gradient_kernel,
        in_specs=[pl.BlockSpec(memory_space=pl.ANY)] + [vmem] * 2,
        out_specs=vmem,
        out_shape=jax.ShapeDtypeStruct((NZ, ROWS, 2 * HD), BF16),
        scratch_shapes=[
            pltpu.VMEM((NZ, ROWS, (NX - 1) * TOKENS), BF16),
            pltpu.SemaphoreType.DMA((2 * (NX - 1),)),
        ],
        compiler_params=pltpu.CompilerParams(vmem_limit_bytes=VMEM_MOST),
        cost_estimate=pl.CostEstimate(
            flops=2 * D * TOKENS * 2 * HD, bytes_accessed=3 * D * TOKENS, transcendentals=0
        ),
        name="gradient",
    )(features, own, scaled)


def hop(a, axis, size, k):
    return lax.ppermute(a, axis, ring(size, k))


def together(*arrays):
    return lax.optimization_barrier(arrays)


def gather_features(shard):
    at_first = lax.axis_index("core") == 0
    x = lax.axis_index("x")
    up = [shard, hop(shard, "y", NY, 1)]
    down = [shard, hop(shard, "y", NY, 7)]
    up[1], down[1], part = together(up[1], down[1], shard)
    first, second = part[:, :L], part[:, L:]
    keep = jnp.where(at_first, first, second)
    come = hop(jnp.where(at_first, second, first), "core", NC, 1)
    up.append(hop(up[1], "y", NY, 1))
    down.append(hop(down[1], "y", NY, 7))
    up[2], down[2], come = together(up[2], down[2], come)
    pair = jnp.where(at_first, jnp.concatenate([keep, come], 0), jnp.concatenate([come, keep], 0))
    piece = lambda k: lax.dynamic_slice_in_dim(pair, lax.rem(x + k, NX) * ROWS, ROWS, 0)
    owned = [hop(piece(NX - k), "x", NX, k) for k in range(1, NX)]
    up.append(hop(up[2], "y", NY, 1))
    down.append(hop(down[2], "y", NY, 7))
    up[3], down[3], *owned = together(up[3], down[3], *owned)
    up.append(hop(up[3], "y", NY, 1))
    owned = lax.all_gather(jnp.stack(owned), ("y", "core"), axis=0)
    return jnp.stack(up + down[:0:-1]), owned.reshape(NY, NC, NX - 1, ROWS, L)


def body(inputs, w_query, w_key, w_value, cotangent, lengths, sampled, step, tree_noise):
    w = jnp.concatenate([w_query, w_key, w_value], 1)
    w = lax.all_gather(w, "x", axis=0, tiled=True)
    w, shard = together(w, inputs.T)
    w = lax.all_gather(w, "z", axis=0, tiled=True)

    mine, owned = gather_features(shard)
    other = hop(mine, "core", NC, 1)
    place = jnp.stack([lax.axis_index(a) for a in ("y", "core", "x")]).astype(jnp.int32)
    gram, own = gram_of(place, mine, other)

    cosine, sine = rope_tables(L, HD)
    grads, norms = attend(
        jnp.concatenate([lengths, sampled]), place, mine, other, w, cotangent, cosine, sine, gram
    )
    grads = [grads] + [hop(grads, "x", NX, k) for k in range(1, NX)]
    norms = lax.psum(norms, "core")
    norms = lax.all_to_all(jnp.broadcast_to(norms, (NX * NY, 4, HD)), ("x", "y"), 0, 0)
    scaled = clip(place, norms.reshape(NX, NY, 4, HD), grads)
    terms = gradient(owned, own, scaled)
    terms = lax.all_to_all(terms, "z", 0, 0)
    summed = jnp.sum(terms.astype(F32), 0)

    levels = tree_noise.shape[0]
    bits = (step[0] // 2 ** jnp.arange(levels, dtype=jnp.int32) % 2).astype(F32)
    noise = jnp.sum(bits[:, None, None, None] * tree_noise, 0)
    expected = 0.85 * (2 * NZ * NX)
    return summed[:, :HD] / expected + noise[0], summed[:, HD:] / expected + noise[1]


def solution(mesh):
    mesh = Mesh(np.asarray(mesh.devices).reshape(NZ, NX, NY, NC), ("z", "x", "y", "core"))
    dp, head = ("z", "x"), ("y", "core")
    in_specs = (
        P(dp, head),
        P(dp, head),
        P(dp, head),
        P(dp, head),
        P(dp, head),
        P(dp),
        P(dp),
        P(),
        P(None, None, dp, head),
    )
    out_specs = (P(dp, head), P(dp, head))
    return jax.shard_map(body, mesh=mesh, in_specs=in_specs, out_specs=out_specs, check_vma=False)
```

```python
import functools
import math

import jax
import jax.numpy as jnp
import numpy as np
from jax import lax
from jax.experimental import pallas as pl
from jax.experimental.pallas import tpu as pltpu
from jax.sharding import Mesh
from jax.sharding import PartitionSpec as P

D = 4608
H = 32
KV = 16
HD = 128
L = 256
NZ, NX, NY, NC = 8, 4, 8, 2
SHARD = D // (NY * NC)
PAIR = NC * SHARD
ROWS = D // (NZ * NX)
TOKENS = 2 * L
CAP = 50.0
SCALE = float(D // H) ** (-0.5)
CLIP = 2.0 * math.sqrt(D * KV * HD)
CHUNK = 2 * PAIR
VMEM = 32 * 1024 * 1024
F32 = jnp.float32
BF16 = jnp.bfloat16

NN = (((1,), (0,)), ((), ()))
NT = (((1,), (1,)), ((), ()))


def dot(a, b, dims=NN):
    return lax.dot_general(a, b, dims, preferred_element_type=F32)


def ring(n, k):
    return [((i + k) % n, i) for i in range(n)]


def rope_tables(length, dim):
    half = dim // 2
    freq = 10000.0 ** (-(jnp.arange(half, dtype=F32) * (2.0 / dim)))
    angle = jnp.arange(length, dtype=F32)[:, None] * freq[None, :]
    cosine = jnp.cos(angle)
    sine = jnp.sin(angle)
    return jnp.concatenate([cosine, cosine], 1), jnp.concatenate([-sine, sine], 1)


def arrange_kernel(place, x_t, x_tok, gram, own):
    for z in range(NZ):
        at = z * PAIR + place[2] * ROWS
        own[z] = x_t[pl.ds(pl.multiple_of(at, ROWS), ROWS)]
    for m in range(NZ // 2):
        parts = []
        for r in (2 * m, 2 * m + 1):
            at = lax.rem(r + place[3], NZ) * PAIR
            parts.append(x_t[pl.ds(pl.multiple_of(at, PAIR), PAIR)])
        rows = jnp.concatenate(parts, 0).T
        x_tok[:, m * CHUNK : (m + 1) * CHUNK] = rows
        for s in range(2):
            part = rows[s * L : (s + 1) * L]
            product = dot(part, part, NT)
            gram[s] = product if m == 0 else gram[s] + product


def arrange(place, x_t):
    vmem = pl.BlockSpec(memory_space=pltpu.VMEM)
    return pl.pallas_call(
        arrange_kernel,
        in_specs=[pl.BlockSpec(memory_space=pltpu.SMEM), vmem],
        out_specs=[vmem] * 3,
        out_shape=[
            jax.ShapeDtypeStruct((TOKENS, D), BF16),
            jax.ShapeDtypeStruct((2, L, L), F32),
            jax.ShapeDtypeStruct((NZ, ROWS, TOKENS), BF16),
        ],
        compiler_params=pltpu.CompilerParams(vmem_limit_bytes=VMEM),
        cost_estimate=pl.CostEstimate(
            flops=2 * 2 * L * L * D, bytes_accessed=2 * 2 * D * TOKENS, transcendentals=0
        ),
        name="arrange",
    )(place, x_t)


def attend_kernel(info, x_tok, *refs):
    w = refs[: NZ + 1]
    cot, cosine, sine, gram, grads, norms, acc = refs[NZ + 1 :]
    blocks = [w[r][...] for r in range(4)]
    blocks += [jnp.concatenate([w[4][...], w[5][...]], 0)]
    blocks += [w[r][...] for r in range(6, 9)]
    for m in range(NZ // 2):
        pair = jnp.concatenate(blocks[2 * m : 2 * m + 2], 0)
        part = dot(x_tok[:, m * CHUNK : (m + 1) * CHUNK], pair)
        acc[...] = part if m == 0 else acc[...] + part

    cos = cosine[...]
    sin = sine[...]
    key_at = lax.broadcasted_iota(jnp.int32, (L, L), 0)
    query_at = lax.broadcasted_iota(jnp.int32, (L, L), 1)
    row_at = lax.broadcasted_iota(jnp.int32, (L, HD), 0)

    def rotated(u):
        return (u * cos + pltpu.roll(u, HD // 2, 1) * sin).astype(BF16)

    for s in range(2):
        rows = slice(s * L, (s + 1) * L)
        length = info[s]
        valid = (row_at < length) & (info[2 + s] > 0)
        keep = (key_at <= query_at) & (key_at < length)
        key = rotated(acc[rows, 2 * HD : 3 * HD])
        value = acc[rows, 3 * HD : 4 * HD].astype(BF16)
        dv = jnp.zeros((L, HD), F32)
        dk_rot = jnp.zeros((L, HD), F32)
        for j in range(2):
            query = rotated(acc[rows, j * HD : (j + 1) * HD])
            grad = jnp.where(valid, cot[rows, j * HD : (j + 1) * HD], jnp.zeros((), BF16))
            bend = jnp.tanh(dot(key, query, NT) * (SCALE / CAP))
            weights = jnp.where(keep, jnp.exp(CAP * bend), 0.0)
            probs = weights * (1.0 / jnp.sum(weights, 0, keepdims=True))
            dv += dot(probs.astype(BF16), grad)
            grad_probs = dot(value, grad, NT)
            delta = jnp.sum(probs * grad_probs, 0, keepdims=True)
            ds = probs * (grad_probs - delta) * ((1.0 - bend * bend) * SCALE)
            dk_rot += dot(ds.astype(BF16), query)
        dk = (dk_rot * cos - pltpu.roll(dk_rot, HD // 2, 1) * sin).astype(BF16)
        dv = dv.astype(BF16)
        for i, d in enumerate((dk, dv)):
            grads[rows, i * HD : (i + 1) * HD] = d
            folded = jnp.sum(gram[s] * dot(d, d, NT), 0, keepdims=True)
            norms[2 * i + s : 2 * i + s + 1] = folded[:, :HD] + folded[:, HD:]


def attend(info, x_tok, w, cot, cosine, sine, gram):
    vmem = pl.BlockSpec(memory_space=pltpu.VMEM)
    return pl.pallas_call(
        attend_kernel,
        in_specs=[pl.BlockSpec(memory_space=pltpu.SMEM)] + [vmem] * (NZ + 6),
        out_specs=[vmem] * 2,
        out_shape=[
            jax.ShapeDtypeStruct((TOKENS, 2 * HD), BF16),
            jax.ShapeDtypeStruct((4, HD), F32),
        ],
        scratch_shapes=[pltpu.VMEM((TOKENS, 4 * HD), F32)],
        compiler_params=pltpu.CompilerParams(vmem_limit_bytes=VMEM),
        cost_estimate=pl.CostEstimate(
            flops=2 * TOKENS * 4 * HD * D + 4 * 12 * L * L * HD,
            bytes_accessed=4 * D * TOKENS,
            transcendentals=8 * L * L,
        ),
        name="attend",
    )(info, x_tok, *w, cot, cosine, sine, gram)


def clip_kernel(place, norms, *refs):
    grads, scaled = refs[:NX], refs[NX]
    for j in range(NX):
        x = lax.rem(place[2] + j, NX)
        sums = jnp.sum(jnp.sum(norms[x], 0), 1, keepdims=True)
        factors = CLIP / jnp.maximum(jnp.sqrt(sums), CLIP)
        for s in range(2):
            rows = slice(s * L, (s + 1) * L)
            for i in range(2):
                columns = slice(i * HD, (i + 1) * HD)
                factor = factors[2 * i + s : 2 * i + s + 1, :]
                part = factor * grads[j][rows, columns].astype(F32)
                scaled[j * TOKENS + s * L : j * TOKENS + (s + 1) * L, columns] = part.astype(BF16)


def clip(place, norms, grads):
    vmem = pl.BlockSpec(memory_space=pltpu.VMEM)
    return pl.pallas_call(
        clip_kernel,
        in_specs=[pl.BlockSpec(memory_space=pltpu.SMEM)] + [vmem] * (NX + 1),
        out_specs=vmem,
        out_shape=jax.ShapeDtypeStruct((NX * TOKENS, 2 * HD), BF16),
        compiler_params=pltpu.CompilerParams(vmem_limit_bytes=VMEM),
        name="clip",
    )(place, norms, *grads)


def gradient_kernel(features, own, scaled, out, held, sems):
    def fetch(j, s):
        columns = pl.ds((2 * (j - 1) + s) * L, L)
        return pltpu.make_async_copy(
            features.at[:, s, j - 1], held.at[:, :, columns], sems.at[2 * (j - 1) + s]
        )

    for j in range(1, NX):
        for s in range(2):
            fetch(j, s).start()
    total = dot(own[...].reshape(NZ * ROWS, TOKENS), scaled[:TOKENS])
    for j in range(1, NX):
        for s in range(2):
            fetch(j, s).wait()
    total += dot(held[...].reshape(NZ * ROWS, (NX - 1) * TOKENS), scaled[TOKENS:])
    out[...] = total.astype(BF16).reshape(NZ, ROWS, 2 * HD)


def gradient(features, own, scaled):
    vmem = pl.BlockSpec(memory_space=pltpu.VMEM)
    return pl.pallas_call(
        gradient_kernel,
        in_specs=[pl.BlockSpec(memory_space=pl.ANY)] + [vmem] * 2,
        out_specs=vmem,
        out_shape=jax.ShapeDtypeStruct((NZ, ROWS, 2 * HD), BF16),
        scratch_shapes=[
            pltpu.VMEM((NZ, ROWS, (NX - 1) * TOKENS), BF16),
            pltpu.SemaphoreType.DMA((2 * (NX - 1),)),
        ],
        compiler_params=pltpu.CompilerParams(vmem_limit_bytes=VMEM),
        cost_estimate=pl.CostEstimate(
            flops=2 * D * TOKENS * 2 * HD, bytes_accessed=3 * D * TOKENS, transcendentals=0
        ),
        name="gradient",
    )(features, own, scaled)


def hop(a, axis, size, k):
    return lax.ppermute(a, axis, ring(size, k))


def together(*arrays):
    return lax.optimization_barrier(arrays)


def gather(w, shard):
    above = lambda a: hop(a, "z", NZ, 1)
    below = lambda a: hop(a, "z", NZ, 7)
    at_first = lax.axis_index("core") == 0
    x = lax.axis_index("x")
    x_t = lax.all_gather(shard, ("y", "core"), axis=0, tiled=True)
    w, part = together(lax.all_gather(w, "x", axis=0, tiled=True), shard)

    first, second = part[:, :L], part[:, L:]
    keep = jnp.where(at_first, first, second)
    come = hop(jnp.where(at_first, second, first), "core", NC, 1)
    v1, e1, come = together(above(w), below(w), come)

    pair = jnp.where(at_first, jnp.concatenate([keep, come], 0), jnp.concatenate([come, keep], 0))
    piece = lambda k: lax.dynamic_slice_in_dim(pair, lax.rem(x + k, NX) * ROWS, ROWS, 0)
    owned = [hop(piece(NX - k), "x", NX, k) for k in range(1, NX)]
    v2, e2, x_t, *owned = together(above(v1), below(e1), x_t, *owned)
    owned = lax.all_gather(jnp.stack(owned), ("y", "core"), axis=0)

    v3, e3 = together(above(v2), below(e2))
    far = [above(v3[:SHARD]), below(e3[SHARD:])]
    return [w, v1, v2, v3, *far, e3, e2, e1], x_t, owned.reshape(NY, NC, NX - 1, ROWS, L)


def body(inputs, w_query, w_key, w_value, cotangent, lengths, sampled, step, tree_noise):
    w = jnp.concatenate([w_query, w_key, w_value], 1)
    w, x_t, owned = gather(w, inputs.T)
    place = jnp.stack([lax.axis_index(a) for a in ("y", "core", "x", "z")]).astype(jnp.int32)
    x_tok, gram, own = arrange(place, x_t)

    cosine, sine = rope_tables(L, HD)
    grads, norms = attend(
        jnp.concatenate([lengths, sampled]), x_tok, w, cotangent, cosine, sine, gram
    )
    grads = [grads] + [hop(grads, "x", NX, k) for k in range(1, NX)]
    norms, owned = together(lax.psum(norms, "core"), owned)
    norms = lax.all_to_all(jnp.broadcast_to(norms, (NX * NY, 4, HD)), ("x", "y"), 0, 0)
    scaled = clip(place, norms.reshape(NX, NY, 4, HD), grads)
    terms = gradient(owned, own, scaled)
    terms = lax.all_to_all(terms, "z", 0, 0)
    summed = jnp.sum(terms.astype(F32), 0)

    levels = tree_noise.shape[0]
    bits = (step[0] // 2 ** jnp.arange(levels, dtype=jnp.int32) % 2).astype(F32)
    noise = jnp.sum(bits[:, None, None, None] * tree_noise, 0)
    expected = 0.85 * (2 * NZ * NX)
    return summed[:, :HD] / expected + noise[0], summed[:, HD:] / expected + noise[1]


def solution(mesh):
    mesh = Mesh(np.asarray(mesh.devices).reshape(NZ, NX, NY, NC), ("z", "x", "y", "core"))
    dp, head = ("z", "x"), ("y", "core")
    in_specs = (
        P(dp, head),
        P(dp, head),
        P(dp, head),
        P(dp, head),
        P(dp, head),
        P(dp),
        P(dp),
        P(),
        P(None, None, dp, head),
    )
    out_specs = (P(dp, head), P(dp, head))
    return jax.shard_map(body, mesh=mesh, in_specs=in_specs, out_specs=out_specs, check_vma=False)
```

```python
import functools
import math

import jax
import jax.numpy as jnp
import numpy as np
from jax import lax
from jax.experimental import pallas as pl
from jax.experimental.pallas import tpu as pltpu
from jax.sharding import Mesh
from jax.sharding import PartitionSpec as P

D = 4608
H = 32
KV = 16
HD = 128
L = 256
NZ, NX, NY, NC = 8, 4, 8, 2
SHARD = D // (NY * NC)
PAIR = NC * SHARD
ROWS = D // (NZ * NX)
TOKENS = 2 * L
CAP = 50.0
SCALE = float(D // H) ** (-0.5)
CLIP = 2.0 * math.sqrt(D * KV * HD)
CHUNK = 2 * PAIR
ORDER = (0, 1, 2, 3, 5, 6, 7, 4)
VMEM = 32 * 1024 * 1024
F32 = jnp.float32
BF16 = jnp.bfloat16

NN = (((1,), (0,)), ((), ()))
NT = (((1,), (1,)), ((), ()))


def dot(a, b, dims=NN):
    return lax.dot_general(a, b, dims, preferred_element_type=F32)


def ring(n, k):
    return [((i + k) % n, i) for i in range(n)]


def rope_tables(length, dim):
    half = dim // 2
    freq = 10000.0 ** (-(jnp.arange(half, dtype=F32) * (2.0 / dim)))
    angle = jnp.arange(length, dtype=F32)[:, None] * freq[None, :]
    cosine = jnp.cos(angle)
    sine = jnp.sin(angle)
    return jnp.concatenate([cosine, cosine], 1), jnp.concatenate([-sine, sine], 1)


def arrange_kernel(place, x_t, x_tok, gram, own):
    for z in range(NZ):
        at = z * PAIR + place[2] * ROWS
        own[z] = x_t[pl.ds(pl.multiple_of(at, ROWS), ROWS)]
    for m in range(NZ // 2):
        parts = []
        for r in ORDER[2 * m : 2 * m + 2]:
            at = lax.rem(r + place[3], NZ) * PAIR
            parts.append(x_t[pl.ds(pl.multiple_of(at, PAIR), PAIR)])
        rows = jnp.concatenate(parts, 0).T
        x_tok[:, m * CHUNK : (m + 1) * CHUNK] = rows
        for s in range(2):
            part = rows[s * L : (s + 1) * L]
            product = dot(part, part, NT)
            gram[s] = product if m == 0 else gram[s] + product


def arrange(place, x_t):
    vmem = pl.BlockSpec(memory_space=pltpu.VMEM)
    return pl.pallas_call(
        arrange_kernel,
        in_specs=[pl.BlockSpec(memory_space=pltpu.SMEM), vmem],
        out_specs=[vmem] * 3,
        out_shape=[
            jax.ShapeDtypeStruct((TOKENS, D), BF16),
            jax.ShapeDtypeStruct((2, L, L), F32),
            jax.ShapeDtypeStruct((NZ, ROWS, TOKENS), BF16),
        ],
        compiler_params=pltpu.CompilerParams(vmem_limit_bytes=VMEM),
        cost_estimate=pl.CostEstimate(
            flops=2 * 2 * L * L * D, bytes_accessed=2 * 2 * D * TOKENS, transcendentals=0
        ),
        name="arrange",
    )(place, x_t)


def project_kernel(x_tok, *refs):
    w, total = refs[: NZ - 2], refs[NZ - 2]
    for m in range(NZ // 2 - 1):
        pair = jnp.concatenate([w[2 * m][...], w[2 * m + 1][...]], 0)
        part = dot(x_tok[:, m * CHUNK : (m + 1) * CHUNK], pair)
        total[...] = part if m == 0 else total[...] + part


def project(x_tok, w):
    vmem = pl.BlockSpec(memory_space=pltpu.VMEM)
    return pl.pallas_call(
        project_kernel,
        in_specs=[vmem] * (NZ - 1),
        out_specs=vmem,
        out_shape=jax.ShapeDtypeStruct((TOKENS, 4 * HD), F32),
        compiler_params=pltpu.CompilerParams(vmem_limit_bytes=VMEM),
        cost_estimate=pl.CostEstimate(
            flops=2 * TOKENS * 3 * HD * D, bytes_accessed=3 * D * TOKENS, transcendentals=0
        ),
        name="project",
    )(x_tok, *w)


def attend_kernel(info, total, x_tok, w, w_a, w_b, cot, cosine, sine, gram, grads, norms, acc):
    pair = jnp.concatenate([w[...], w_a[...], w_b[...]], 0)
    acc[...] = total[...] + dot(x_tok[:, D - CHUNK :], pair)

    cos = cosine[...]
    sin = sine[...]
    key_at = lax.broadcasted_iota(jnp.int32, (L, L), 0)
    query_at = lax.broadcasted_iota(jnp.int32, (L, L), 1)
    row_at = lax.broadcasted_iota(jnp.int32, (L, HD), 0)

    def rotated(u):
        return (u * cos + pltpu.roll(u, HD // 2, 1) * sin).astype(BF16)

    for s in range(2):
        rows = slice(s * L, (s + 1) * L)
        length = info[s]
        valid = (row_at < length) & (info[2 + s] > 0)
        keep = (key_at <= query_at) & (key_at < length)
        key = rotated(acc[rows, 2 * HD : 3 * HD])
        value = acc[rows, 3 * HD : 4 * HD].astype(BF16)
        dv = jnp.zeros((L, HD), F32)
        dk_rot = jnp.zeros((L, HD), F32)
        for j in range(2):
            query = rotated(acc[rows, j * HD : (j + 1) * HD])
            grad = jnp.where(valid, cot[rows, j * HD : (j + 1) * HD], jnp.zeros((), BF16))
            bend = jnp.tanh(dot(key, query, NT) * (SCALE / CAP))
            weights = jnp.where(keep, jnp.exp(CAP * bend), 0.0)
            probs = weights * (1.0 / jnp.sum(weights, 0, keepdims=True))
            dv += dot(probs.astype(BF16), grad)
            grad_probs = dot(value, grad, NT)
            delta = jnp.sum(probs * grad_probs, 0, keepdims=True)
            ds = probs * (grad_probs - delta) * ((1.0 - bend * bend) * SCALE)
            dk_rot += dot(ds.astype(BF16), query)
        dk = (dk_rot * cos - pltpu.roll(dk_rot, HD // 2, 1) * sin).astype(BF16)
        dv = dv.astype(BF16)
        for i, d in enumerate((dk, dv)):
            grads[rows, i * HD : (i + 1) * HD] = d
            folded = jnp.sum(gram[s] * dot(d, d, NT), 0, keepdims=True)
            norms[2 * i + s : 2 * i + s + 1] = folded[:, :HD] + folded[:, HD:]


def attend(info, total, x_tok, w, cot, cosine, sine, gram):
    vmem = pl.BlockSpec(memory_space=pltpu.VMEM)
    return pl.pallas_call(
        attend_kernel,
        in_specs=[pl.BlockSpec(memory_space=pltpu.SMEM)] + [vmem] * 9,
        out_specs=[vmem] * 2,
        out_shape=[
            jax.ShapeDtypeStruct((TOKENS, 2 * HD), BF16),
            jax.ShapeDtypeStruct((4, HD), F32),
        ],
        scratch_shapes=[pltpu.VMEM((TOKENS, 4 * HD), F32)],
        compiler_params=pltpu.CompilerParams(vmem_limit_bytes=VMEM),
        cost_estimate=pl.CostEstimate(
            flops=2 * TOKENS * 4 * HD * D + 4 * 12 * L * L * HD,
            bytes_accessed=4 * D * TOKENS,
            transcendentals=8 * L * L,
        ),
        name="attend",
    )(info, total, x_tok, *w, cot, cosine, sine, gram)


def clip_kernel(place, norms, *refs):
    grads, scaled = refs[:NX], refs[NX]
    for j in range(NX):
        x = lax.rem(place[2] + j, NX)
        sums = jnp.sum(jnp.sum(norms[x], 0), 1, keepdims=True)
        factors = CLIP / jnp.maximum(jnp.sqrt(sums), CLIP)
        for s in range(2):
            rows = slice(s * L, (s + 1) * L)
            for i in range(2):
                columns = slice(i * HD, (i + 1) * HD)
                factor = factors[2 * i + s : 2 * i + s + 1, :]
                part = factor * grads[j][rows, columns].astype(F32)
                scaled[j * TOKENS + s * L : j * TOKENS + (s + 1) * L, columns] = part.astype(BF16)


def clip(place, norms, grads):
    vmem = pl.BlockSpec(memory_space=pltpu.VMEM)
    return pl.pallas_call(
        clip_kernel,
        in_specs=[pl.BlockSpec(memory_space=pltpu.SMEM)] + [vmem] * (NX + 1),
        out_specs=vmem,
        out_shape=jax.ShapeDtypeStruct((NX * TOKENS, 2 * HD), BF16),
        compiler_params=pltpu.CompilerParams(vmem_limit_bytes=VMEM),
        name="clip",
    )(place, norms, *grads)


def stage_kernel(features, out, sems):
    def fetch(j, s):
        columns = pl.ds((2 * (j - 1) + s) * L, L)
        return pltpu.make_async_copy(
            features.at[:, s, j - 1], out.at[:, :, columns], sems.at[2 * (j - 1) + s]
        )

    for j in range(1, NX):
        for s in range(2):
            fetch(j, s).start()
    for j in range(1, NX):
        for s in range(2):
            fetch(j, s).wait()


def stage(features):
    return pl.pallas_call(
        stage_kernel,
        in_specs=[pl.BlockSpec(memory_space=pl.ANY)],
        out_specs=pl.BlockSpec(memory_space=pltpu.VMEM),
        out_shape=jax.ShapeDtypeStruct((NZ, ROWS, (NX - 1) * TOKENS), BF16),
        scratch_shapes=[pltpu.SemaphoreType.DMA((2 * (NX - 1),))],
        compiler_params=pltpu.CompilerParams(vmem_limit_bytes=VMEM),
        cost_estimate=pl.CostEstimate(flops=0, bytes_accessed=4 * D * TOKENS, transcendentals=0),
        name="stage",
    )(features)


def gradient_kernel(staged, own, scaled, out):
    total = dot(own[...].reshape(NZ * ROWS, TOKENS), scaled[:TOKENS])
    total += dot(staged[...].reshape(NZ * ROWS, (NX - 1) * TOKENS), scaled[TOKENS:])
    out[...] = total.astype(BF16).reshape(NZ, ROWS, 2 * HD)


def gradient(staged, own, scaled):
    vmem = pl.BlockSpec(memory_space=pltpu.VMEM)
    return pl.pallas_call(
        gradient_kernel,
        in_specs=[vmem] * 3,
        out_specs=vmem,
        out_shape=jax.ShapeDtypeStruct((NZ, ROWS, 2 * HD), BF16),
        compiler_params=pltpu.CompilerParams(vmem_limit_bytes=VMEM),
        cost_estimate=pl.CostEstimate(
            flops=2 * D * TOKENS * 2 * HD, bytes_accessed=3 * D * TOKENS, transcendentals=0
        ),
        name="gradient",
    )(staged, own, scaled)


def hop(a, axis, size, k):
    return lax.ppermute(a, axis, ring(size, k))


def together(*arrays):
    return lax.optimization_barrier(arrays)


def gather(w, shard):
    above = lambda a: hop(a, "z", NZ, 1)
    below = lambda a: hop(a, "z", NZ, 7)
    at_first = lax.axis_index("core") == 0
    x = lax.axis_index("x")
    x_t = lax.all_gather(shard, ("y", "core"), axis=0, tiled=True)
    w, part = together(lax.all_gather(w, "x", axis=0, tiled=True), shard)

    first, second = part[:, :L], part[:, L:]
    keep = jnp.where(at_first, first, second)
    come = hop(jnp.where(at_first, second, first), "core", NC, 1)
    v1, e1, come = together(above(w), below(w), come)

    pair = jnp.where(at_first, jnp.concatenate([keep, come], 0), jnp.concatenate([come, keep], 0))
    piece = lambda k: lax.dynamic_slice_in_dim(pair, lax.rem(x + k, NX) * ROWS, ROWS, 0)
    owned = [hop(piece(NX - k), "x", NX, k) for k in range(1, NX)]
    v2, e2, x_t, *owned = together(above(v1), below(e1), x_t, *owned)
    owned = lax.all_gather(jnp.stack(owned), ("y", "core"), axis=0)

    v3, e3 = together(above(v2), below(e2))
    place = jnp.stack([lax.axis_index(a) for a in ("y", "core", "x", "z")]).astype(jnp.int32)
    x_tok, gram, own = arrange(place, x_t)
    v3, e3, gram = together(v3, e3, gram)
    far = [above(v3[:SHARD]), below(e3[SHARD:])]
    total = project(x_tok, [w, v1, v2, v3, e3, e2])
    owned = owned.reshape(NY, NC, NX - 1, ROWS, L)
    return total, x_tok, [e1, *far], gram, own, owned, place


def body(inputs, w_query, w_key, w_value, cotangent, lengths, sampled, step, tree_noise):
    w = jnp.concatenate([w_query, w_key, w_value], 1)
    total, x_tok, w, gram, own, owned, place = gather(w, inputs.T)

    cosine, sine = rope_tables(L, HD)
    grads, norms = attend(
        jnp.concatenate([lengths, sampled]), total, x_tok, w, cotangent, cosine, sine, gram
    )
    grads = [grads] + [hop(grads, "x", NX, k) for k in range(1, NX)]
    norms, owned = together(lax.psum(norms, "core"), owned)
    norms = lax.all_to_all(jnp.broadcast_to(norms, (NX * NY, 4, HD)), ("x", "y"), 0, 0)
    scaled = clip(place, norms.reshape(NX, NY, 4, HD), grads)
    terms = gradient(stage(owned), own, scaled)
    terms = lax.all_to_all(terms, "z", 0, 0)
    summed = jnp.sum(terms.astype(F32), 0)

    levels = tree_noise.shape[0]
    bits = (step[0] // 2 ** jnp.arange(levels, dtype=jnp.int32) % 2).astype(F32)
    noise = jnp.sum(bits[:, None, None, None] * tree_noise, 0)
    expected = 0.85 * (2 * NZ * NX)
    return summed[:, :HD] / expected + noise[0], summed[:, HD:] / expected + noise[1]


def solution(mesh):
    mesh = Mesh(np.asarray(mesh.devices).reshape(NZ, NX, NY, NC), ("z", "x", "y", "core"))
    dp, head = ("z", "x"), ("y", "core")
    in_specs = (
        P(dp, head),
        P(dp, head),
        P(dp, head),
        P(dp, head),
        P(dp, head),
        P(dp),
        P(dp),
        P(),
        P(None, None, dp, head),
    )
    out_specs = (P(dp, head), P(dp, head))
    return jax.shard_map(body, mesh=mesh, in_specs=in_specs, out_specs=out_specs, check_vma=False)
```

```python
import functools
import math

import jax
import jax.numpy as jnp
import numpy as np
from jax import lax
from jax.experimental import pallas as pl
from jax.experimental.pallas import tpu as pltpu
from jax.sharding import Mesh
from jax.sharding import PartitionSpec as P

D = 4608
H = 32
KV = 16
HD = 128
L = 256
NZ, NX, NY, NC = 8, 4, 8, 2
SHARD = D // (NY * NC)
PAIR = NC * SHARD
ROWS = D // (NZ * NX)
TOKENS = 2 * L
CAP = 50.0
SCALE = float(D // H) ** (-0.5)
CLIP = 2.0 * math.sqrt(D * KV * HD)
CHUNK = 2 * PAIR
ORDER = (0, 1, 2, 3, 5, 6, 7, 4)
VMEM = 32 * 1024 * 1024
F32 = jnp.float32
BF16 = jnp.bfloat16

NN = (((1,), (0,)), ((), ()))
NT = (((1,), (1,)), ((), ()))


def dot(a, b, dims=NN):
    return lax.dot_general(a, b, dims, preferred_element_type=F32)


def ring(n, k):
    return [((i + k) % n, i) for i in range(n)]


def rope_tables(length, dim):
    half = dim // 2
    freq = 10000.0 ** (-(jnp.arange(half, dtype=F32) * (2.0 / dim)))
    angle = jnp.arange(length, dtype=F32)[:, None] * freq[None, :]
    cosine = jnp.cos(angle)
    sine = jnp.sin(angle)
    return jnp.concatenate([cosine, cosine], 1), jnp.concatenate([-sine, sine], 1)


def arrange_kernel(place, x_t, x_tok, gram, own):
    for z in range(NZ):
        at = z * PAIR + place[2] * ROWS
        own[z] = x_t[pl.ds(pl.multiple_of(at, ROWS), ROWS)]
    for m in range(NZ // 2):
        parts = []
        for r in ORDER[2 * m : 2 * m + 2]:
            at = lax.rem(r + place[3], NZ) * PAIR
            parts.append(x_t[pl.ds(pl.multiple_of(at, PAIR), PAIR)])
        rows = jnp.concatenate(parts, 0).T
        x_tok[:, m * CHUNK : (m + 1) * CHUNK] = rows
        for s in range(2):
            part = rows[s * L : (s + 1) * L]
            product = dot(part, part, NT)
            gram[s] = product if m == 0 else gram[s] + product


def arrange(place, x_t):
    vmem = pl.BlockSpec(memory_space=pltpu.VMEM)
    return pl.pallas_call(
        arrange_kernel,
        in_specs=[pl.BlockSpec(memory_space=pltpu.SMEM), vmem],
        out_specs=[vmem] * 3,
        out_shape=[
            jax.ShapeDtypeStruct((TOKENS, D), BF16),
            jax.ShapeDtypeStruct((2, L, L), F32),
            jax.ShapeDtypeStruct((NZ, ROWS, TOKENS), BF16),
        ],
        compiler_params=pltpu.CompilerParams(vmem_limit_bytes=VMEM),
        cost_estimate=pl.CostEstimate(
            flops=2 * 2 * L * L * D, bytes_accessed=2 * 2 * D * TOKENS, transcendentals=0
        ),
        name="arrange",
    )(place, x_t)


def project_kernel(x_tok, *refs):
    w, total = refs[: NZ - 2], refs[NZ - 2]
    for m in range(NZ // 2 - 1):
        pair = jnp.concatenate([w[2 * m][...], w[2 * m + 1][...]], 0)
        part = dot(x_tok[:, m * CHUNK : (m + 1) * CHUNK], pair)
        total[...] = part if m == 0 else total[...] + part


def project(x_tok, w):
    vmem = pl.BlockSpec(memory_space=pltpu.VMEM)
    return pl.pallas_call(
        project_kernel,
        in_specs=[vmem] * (NZ - 1),
        out_specs=vmem,
        out_shape=jax.ShapeDtypeStruct((TOKENS, 4 * HD), F32),
        compiler_params=pltpu.CompilerParams(vmem_limit_bytes=VMEM),
        cost_estimate=pl.CostEstimate(
            flops=2 * TOKENS * 3 * HD * D, bytes_accessed=3 * D * TOKENS, transcendentals=0
        ),
        name="project",
    )(x_tok, *w)


def attend_kernel(info, total, x_tok, w, w_a, w_b, cot, cosine, sine, gram, grads, norms, acc):
    pair = jnp.concatenate([w[...], w_a[...], w_b[...]], 0)
    acc[...] = total[...] + dot(x_tok[:, D - CHUNK :], pair)

    cos = cosine[...]
    sin = sine[...]
    key_at = lax.broadcasted_iota(jnp.int32, (L, L), 0)
    query_at = lax.broadcasted_iota(jnp.int32, (L, L), 1)
    row_at = lax.broadcasted_iota(jnp.int32, (L, HD), 0)

    def rotated(u):
        return (u * cos + pltpu.roll(u, HD // 2, 1) * sin).astype(BF16)

    for s in range(2):
        rows = slice(s * L, (s + 1) * L)
        length = info[s]
        valid = (row_at < length) & (info[2 + s] > 0)
        keep = (key_at <= query_at) & (key_at < length)
        key = rotated(acc[rows, 2 * HD : 3 * HD])
        value = acc[rows, 3 * HD : 4 * HD].astype(BF16)
        dv = jnp.zeros((L, HD), F32)
        dk_rot = jnp.zeros((L, HD), F32)
        for j in range(2):
            query = rotated(acc[rows, j * HD : (j + 1) * HD])
            grad = jnp.where(valid, cot[rows, j * HD : (j + 1) * HD], jnp.zeros((), BF16))
            bend = jnp.tanh(dot(key, query, NT) * (SCALE / CAP))
            weights = jnp.where(keep, jnp.exp(CAP * bend), 0.0)
            probs = weights * (1.0 / jnp.sum(weights, 0, keepdims=True))
            dv += dot(probs.astype(BF16), grad)
            grad_probs = dot(value, grad, NT)
            delta = jnp.sum(probs * grad_probs, 0, keepdims=True)
            ds = probs * (grad_probs - delta) * ((1.0 - bend * bend) * SCALE)
            dk_rot += dot(ds.astype(BF16), query)
        dk = (dk_rot * cos - pltpu.roll(dk_rot, HD // 2, 1) * sin).astype(BF16)
        dv = dv.astype(BF16)
        for i, d in enumerate((dk, dv)):
            grads[rows, i * HD : (i + 1) * HD] = d
            folded = jnp.sum(gram[s] * dot(d, d, NT), 0, keepdims=True)
            norms[2 * i + s : 2 * i + s + 1] = folded[:, :HD] + folded[:, HD:]


def attend(info, total, x_tok, w, cot, cosine, sine, gram):
    vmem = pl.BlockSpec(memory_space=pltpu.VMEM)
    return pl.pallas_call(
        attend_kernel,
        in_specs=[pl.BlockSpec(memory_space=pltpu.SMEM)] + [vmem] * 9,
        out_specs=[vmem] * 2,
        out_shape=[
            jax.ShapeDtypeStruct((TOKENS, 2 * HD), BF16),
            jax.ShapeDtypeStruct((4, HD), F32),
        ],
        scratch_shapes=[pltpu.VMEM((TOKENS, 4 * HD), F32)],
        compiler_params=pltpu.CompilerParams(vmem_limit_bytes=VMEM),
        cost_estimate=pl.CostEstimate(
            flops=2 * TOKENS * 4 * HD * D + 4 * 12 * L * L * HD,
            bytes_accessed=4 * D * TOKENS,
            transcendentals=8 * L * L,
        ),
        name="attend",
    )(info, total, x_tok, *w, cot, cosine, sine, gram)


def clip_kernel(place, norms, *refs):
    grads, scaled = refs[:NX], refs[NX]
    for j in range(NX):
        x = lax.rem(place[2] + j, NX)
        sums = jnp.sum(jnp.sum(norms[x], 0), 1, keepdims=True)
        factors = CLIP / jnp.maximum(jnp.sqrt(sums), CLIP)
        for s in range(2):
            rows = slice(s * L, (s + 1) * L)
            for i in range(2):
                columns = slice(i * HD, (i + 1) * HD)
                factor = factors[2 * i + s : 2 * i + s + 1, :]
                part = factor * grads[j][rows, columns].astype(F32)
                scaled[j * TOKENS + s * L : j * TOKENS + (s + 1) * L, columns] = part.astype(BF16)


def clip(place, norms, grads):
    vmem = pl.BlockSpec(memory_space=pltpu.VMEM)
    return pl.pallas_call(
        clip_kernel,
        in_specs=[pl.BlockSpec(memory_space=pltpu.SMEM)] + [vmem] * (NX + 1),
        out_specs=vmem,
        out_shape=jax.ShapeDtypeStruct((NX * TOKENS, 2 * HD), BF16),
        compiler_params=pltpu.CompilerParams(vmem_limit_bytes=VMEM),
        name="clip",
    )(place, norms, *grads)


def stage_kernel(features, out, sems):
    def fetch(j, s):
        columns = pl.ds((2 * (j - 1) + s) * L, L)
        return pltpu.make_async_copy(
            features.at[:, s, j - 1], out.at[:, :, columns], sems.at[2 * (j - 1) + s]
        )

    for j in range(1, NX):
        for s in range(2):
            fetch(j, s).start()
    for j in range(1, NX):
        for s in range(2):
            fetch(j, s).wait()


def stage(features):
    return pl.pallas_call(
        stage_kernel,
        in_specs=[pl.BlockSpec(memory_space=pl.ANY)],
        out_specs=pl.BlockSpec(memory_space=pltpu.VMEM),
        out_shape=jax.ShapeDtypeStruct((NZ, ROWS, (NX - 1) * TOKENS), BF16),
        scratch_shapes=[pltpu.SemaphoreType.DMA((2 * (NX - 1),))],
        compiler_params=pltpu.CompilerParams(vmem_limit_bytes=VMEM),
        cost_estimate=pl.CostEstimate(flops=0, bytes_accessed=4 * D * TOKENS, transcendentals=0),
        name="stage",
    )(features)


def gradient_kernel(staged, own, scaled, out):
    total = dot(own[...].reshape(NZ * ROWS, TOKENS), scaled[:TOKENS])
    total += dot(staged[...].reshape(NZ * ROWS, (NX - 1) * TOKENS), scaled[TOKENS:])
    out[...] = total.astype(BF16).reshape(NZ, ROWS, 2 * HD)


def gradient(staged, own, scaled):
    vmem = pl.BlockSpec(memory_space=pltpu.VMEM)
    return pl.pallas_call(
        gradient_kernel,
        in_specs=[vmem] * 3,
        out_specs=vmem,
        out_shape=jax.ShapeDtypeStruct((NZ, ROWS, 2 * HD), BF16),
        compiler_params=pltpu.CompilerParams(vmem_limit_bytes=VMEM),
        cost_estimate=pl.CostEstimate(
            flops=2 * D * TOKENS * 2 * HD, bytes_accessed=3 * D * TOKENS, transcendentals=0
        ),
        name="gradient",
    )(staged, own, scaled)


def hop(a, axis, size, k):
    return lax.ppermute(a, axis, ring(size, k))


def together(*arrays):
    return lax.optimization_barrier(arrays)


def gather(w, shard):
    above = lambda a: hop(a, "z", NZ, 1)
    below = lambda a: hop(a, "z", NZ, 7)
    at_first = lax.axis_index("core") == 0
    x = lax.axis_index("x")
    x_t = lax.all_gather(shard, ("y", "core"), axis=0, tiled=True)
    w, part = together(lax.all_gather(w, "x", axis=0, tiled=True), shard)

    first, second = part[:, :L], part[:, L:]
    keep = jnp.where(at_first, first, second)
    come = hop(jnp.where(at_first, second, first), "core", NC, 1)
    v1, e1, come = together(above(w), below(w), come)

    pair = jnp.where(at_first, jnp.concatenate([keep, come], 0), jnp.concatenate([come, keep], 0))
    owned = lax.all_to_all(pair.reshape(NX, ROWS, L), "x", 0, 0)
    v2, e2, x_t, owned = together(above(v1), below(e1), x_t, owned)
    owned = jnp.stack([lax.dynamic_index_in_dim(owned, lax.rem(x + j, NX), 0, False) for j in range(1, NX)])
    owned = lax.all_gather(owned, ("y", "core"), axis=0)

    v3, e3 = together(above(v2), below(e2))
    place = jnp.stack([lax.axis_index(a) for a in ("y", "core", "x", "z")]).astype(jnp.int32)
    x_tok, gram, own = arrange(place, x_t)
    v3, e3, gram = together(v3, e3, gram)
    far = [above(v3[:SHARD]), below(e3[SHARD:])]
    total = project(x_tok, [w, v1, v2, v3, e3, e2])
    owned = owned.reshape(NY, NC, NX - 1, ROWS, L)
    return total, x_tok, [e1, *far], gram, own, owned, place


def body(inputs, w_query, w_key, w_value, cotangent, lengths, sampled, step, tree_noise):
    w = jnp.concatenate([w_query, w_key, w_value], 1)
    total, x_tok, w, gram, own, owned, place = gather(w, inputs.T)

    cosine, sine = rope_tables(L, HD)
    grads, norms = attend(
        jnp.concatenate([lengths, sampled]), total, x_tok, w, cotangent, cosine, sine, gram
    )
    grads = [grads] + [hop(grads, "x", NX, k) for k in range(1, NX)]
    norms, owned = together(lax.psum(norms, "core"), owned)
    norms = lax.all_to_all(jnp.broadcast_to(norms, (NX * NY, 4, HD)), ("x", "y"), 0, 0)
    scaled = clip(place, norms.reshape(NX, NY, 4, HD), grads)
    terms = gradient(stage(owned), own, scaled)
    terms = lax.all_to_all(terms, "z", 0, 0)
    summed = jnp.sum(terms.astype(F32), 0)

    levels = tree_noise.shape[0]
    bits = (step[0] // 2 ** jnp.arange(levels, dtype=jnp.int32) % 2).astype(F32)
    noise = jnp.sum(bits[:, None, None, None] * tree_noise, 0)
    expected = 0.85 * (2 * NZ * NX)
    return summed[:, :HD] / expected + noise[0], summed[:, HD:] / expected + noise[1]


def solution(mesh):
    mesh = Mesh(np.asarray(mesh.devices).reshape(NZ, NX, NY, NC), ("z", "x", "y", "core"))
    dp, head = ("z", "x"), ("y", "core")
    in_specs = (
        P(dp, head),
        P(dp, head),
        P(dp, head),
        P(dp, head),
        P(dp, head),
        P(dp),
        P(dp),
        P(),
        P(None, None, dp, head),
    )
    out_specs = (P(dp, head), P(dp, head))
    return jax.shard_map(body, mesh=mesh, in_specs=in_specs, out_specs=out_specs, check_vma=False)
```

```python
import functools
import math

import jax
import jax.numpy as jnp
import numpy as np
from jax import lax
from jax.experimental import pallas as pl
from jax.experimental.pallas import tpu as pltpu
from jax.sharding import Mesh
from jax.sharding import PartitionSpec as P

D = 4608
H = 32
KV = 16
HD = 128
L = 256
NZ, NX, NY, NC = 8, 4, 8, 2
SHARD = D // (NY * NC)
PAIR = NC * SHARD
ROWS = D // (NZ * NX)
TOKENS = 2 * L
CAP = 50.0
SCALE = float(D // H) ** (-0.5)
CLIP = 2.0 * math.sqrt(D * KV * HD)
CHUNK = 2 * PAIR
ORDER = (0, 1, 2, 3, 5, 6, 7, 4)
VMEM = 32 * 1024 * 1024
F32 = jnp.float32
BF16 = jnp.bfloat16

NN = (((1,), (0,)), ((), ()))
NT = (((1,), (1,)), ((), ()))


def dot(a, b, dims=NN):
    return lax.dot_general(a, b, dims, preferred_element_type=F32)


def ring(n, k):
    return [((i + k) % n, i) for i in range(n)]


def rope_tables(length, dim):
    half = dim // 2
    freq = 10000.0 ** (-(jnp.arange(half, dtype=F32) * (2.0 / dim)))
    angle = jnp.arange(length, dtype=F32)[:, None] * freq[None, :]
    cosine = jnp.cos(angle)
    sine = jnp.sin(angle)
    return jnp.concatenate([cosine, cosine], 1), jnp.concatenate([-sine, sine], 1)


def arrange_kernel(place, x_t, x_tok, gram, own):
    for z in range(NZ):
        at = z * PAIR + place[2] * ROWS
        own[z] = x_t[pl.ds(pl.multiple_of(at, ROWS), ROWS)]
    for m in range(NZ // 2):
        parts = []
        for r in ORDER[2 * m : 2 * m + 2]:
            at = lax.rem(r + place[3], NZ) * PAIR
            parts.append(x_t[pl.ds(pl.multiple_of(at, PAIR), PAIR)])
        rows = jnp.concatenate(parts, 0).T
        x_tok[:, m * CHUNK : (m + 1) * CHUNK] = rows
        for s in range(2):
            part = rows[s * L : (s + 1) * L]
            product = dot(part, part, NT)
            gram[s] = product if m == 0 else gram[s] + product


def arrange(place, x_t):
    vmem = pl.BlockSpec(memory_space=pltpu.VMEM)
    return pl.pallas_call(
        arrange_kernel,
        in_specs=[pl.BlockSpec(memory_space=pltpu.SMEM), vmem],
        out_specs=[vmem] * 3,
        out_shape=[
            jax.ShapeDtypeStruct((TOKENS, D), BF16),
            jax.ShapeDtypeStruct((2, L, L), F32),
            jax.ShapeDtypeStruct((NZ, ROWS, TOKENS), BF16),
        ],
        compiler_params=pltpu.CompilerParams(vmem_limit_bytes=VMEM),
        cost_estimate=pl.CostEstimate(
            flops=2 * 2 * L * L * D, bytes_accessed=2 * 2 * D * TOKENS, transcendentals=0
        ),
        name="arrange",
    )(place, x_t)


def project_kernel(x_tok, *refs):
    w, total = refs[: NZ - 2], refs[NZ - 2]
    for m in range(NZ // 2 - 1):
        pair = jnp.concatenate([w[2 * m][...], w[2 * m + 1][...]], 0)
        part = dot(x_tok[:, m * CHUNK : (m + 1) * CHUNK], pair)
        total[...] = part if m == 0 else total[...] + part


def project(x_tok, w):
    vmem = pl.BlockSpec(memory_space=pltpu.VMEM)
    return pl.pallas_call(
        project_kernel,
        in_specs=[vmem] * (NZ - 1),
        out_specs=vmem,
        out_shape=jax.ShapeDtypeStruct((TOKENS, 4 * HD), F32),
        compiler_params=pltpu.CompilerParams(vmem_limit_bytes=VMEM),
        cost_estimate=pl.CostEstimate(
            flops=2 * TOKENS * 3 * HD * D, bytes_accessed=3 * D * TOKENS, transcendentals=0
        ),
        name="project",
    )(x_tok, *w)


def attend_kernel(info, total, x_tok, w, w_a, w_b, cot, cosine, sine, gram, grads, norms, acc):
    pair = jnp.concatenate([w[...], w_a[...], w_b[...]], 0)
    acc[...] = total[...] + dot(x_tok[:, D - CHUNK :], pair)

    cos = cosine[...]
    sin = sine[...]
    key_at = lax.broadcasted_iota(jnp.int32, (L, L), 0)
    query_at = lax.broadcasted_iota(jnp.int32, (L, L), 1)
    row_at = lax.broadcasted_iota(jnp.int32, (L, HD), 0)

    def rotated(u):
        return (u * cos + pltpu.roll(u, HD // 2, 1) * sin).astype(BF16)

    for s in range(2):
        rows = slice(s * L, (s + 1) * L)
        length = info[s]
        valid = (row_at < length) & (info[2 + s] > 0)
        keep = (key_at <= query_at) & (key_at < length)
        key = rotated(acc[rows, 2 * HD : 3 * HD])
        value = acc[rows, 3 * HD : 4 * HD].astype(BF16)
        dv = jnp.zeros((L, HD), F32)
        dk_rot = jnp.zeros((L, HD), F32)
        for j in range(2):
            query = rotated(acc[rows, j * HD : (j + 1) * HD])
            grad = jnp.where(valid, cot[rows, j * HD : (j + 1) * HD], jnp.zeros((), BF16))
            bend = jnp.tanh(dot(key, query, NT) * (SCALE / CAP))
            weights = jnp.where(keep, jnp.exp(CAP * bend), 0.0)
            probs = weights * (1.0 / jnp.sum(weights, 0, keepdims=True))
            dv += dot(probs.astype(BF16), grad)
            grad_probs = dot(value, grad, NT)
            delta = jnp.sum(probs * grad_probs, 0, keepdims=True)
            ds = probs * (grad_probs - delta) * ((1.0 - bend * bend) * SCALE)
            dk_rot += dot(ds.astype(BF16), query)
        dk = (dk_rot * cos - pltpu.roll(dk_rot, HD // 2, 1) * sin).astype(BF16)
        dv = dv.astype(BF16)
        for i, d in enumerate((dk, dv)):
            grads[rows, i * HD : (i + 1) * HD] = d
            folded = jnp.sum(gram[s] * dot(d, d, NT), 0, keepdims=True)
            norms[2 * i + s : 2 * i + s + 1] = folded[:, :HD] + folded[:, HD:]


def attend(info, total, x_tok, w, cot, cosine, sine, gram):
    vmem = pl.BlockSpec(memory_space=pltpu.VMEM)
    return pl.pallas_call(
        attend_kernel,
        in_specs=[pl.BlockSpec(memory_space=pltpu.SMEM)] + [vmem] * 9,
        out_specs=[vmem] * 2,
        out_shape=[
            jax.ShapeDtypeStruct((TOKENS, 2 * HD), BF16),
            jax.ShapeDtypeStruct((4, HD), F32),
        ],
        scratch_shapes=[pltpu.VMEM((TOKENS, 4 * HD), F32)],
        compiler_params=pltpu.CompilerParams(vmem_limit_bytes=VMEM),
        cost_estimate=pl.CostEstimate(
            flops=2 * TOKENS * 4 * HD * D + 4 * 12 * L * L * HD,
            bytes_accessed=4 * D * TOKENS,
            transcendentals=8 * L * L,
        ),
        name="attend",
    )(info, total, x_tok, *w, cot, cosine, sine, gram)


def stage_kernel(features, out, sems):
    def fetch(j, s):
        columns = pl.ds((2 * (j - 1) + s) * L, L)
        return pltpu.make_async_copy(
            features.at[:, s, j - 1], out.at[:, :, columns], sems.at[2 * (j - 1) + s]
        )

    for j in range(1, NX):
        for s in range(2):
            fetch(j, s).start()
    for j in range(1, NX):
        for s in range(2):
            fetch(j, s).wait()


def stage(features):
    return pl.pallas_call(
        stage_kernel,
        in_specs=[pl.BlockSpec(memory_space=pl.ANY)],
        out_specs=pl.BlockSpec(memory_space=pltpu.VMEM),
        out_shape=jax.ShapeDtypeStruct((NZ, ROWS, (NX - 1) * TOKENS), BF16),
        scratch_shapes=[pltpu.SemaphoreType.DMA((2 * (NX - 1),))],
        compiler_params=pltpu.CompilerParams(vmem_limit_bytes=VMEM),
        cost_estimate=pl.CostEstimate(flops=0, bytes_accessed=4 * D * TOKENS, transcendentals=0),
        name="stage",
    )(features)


def gradient_kernel(place, norms, staged, own, *refs):
    grads, (out, scaled) = refs[:NX], refs[NX:]
    for j in range(NX):
        x = lax.rem(place[2] + j, NX)
        sums = jnp.sum(jnp.sum(norms[x], 0), 1, keepdims=True)
        factors = CLIP / jnp.maximum(jnp.sqrt(sums), CLIP)
        for s in range(2):
            rows = slice(s * L, (s + 1) * L)
            for i in range(2):
                columns = slice(i * HD, (i + 1) * HD)
                factor = factors[2 * i + s : 2 * i + s + 1, :]
                part = factor * grads[j][rows, columns].astype(F32)
                scaled[j * TOKENS + s * L : j * TOKENS + (s + 1) * L, columns] = part.astype(BF16)
    total = dot(own[...].reshape(NZ * ROWS, TOKENS), scaled[:TOKENS])
    total += dot(staged[...].reshape(NZ * ROWS, (NX - 1) * TOKENS), scaled[TOKENS:])
    out[...] = total.astype(BF16).reshape(NZ, ROWS, 2 * HD)


def gradient(place, norms, staged, own, grads):
    vmem = pl.BlockSpec(memory_space=pltpu.VMEM)
    return pl.pallas_call(
        gradient_kernel,
        in_specs=[pl.BlockSpec(memory_space=pltpu.SMEM)] + [vmem] * (NX + 3),
        out_specs=vmem,
        out_shape=jax.ShapeDtypeStruct((NZ, ROWS, 2 * HD), BF16),
        scratch_shapes=[pltpu.VMEM((NX * TOKENS, 2 * HD), BF16)],
        compiler_params=pltpu.CompilerParams(vmem_limit_bytes=VMEM),
        cost_estimate=pl.CostEstimate(
            flops=2 * D * TOKENS * 2 * HD, bytes_accessed=3 * D * TOKENS, transcendentals=0
        ),
        name="gradient",
    )(place, norms, staged, own, *grads)


def hop(a, axis, size, k):
    return lax.ppermute(a, axis, ring(size, k))


def together(*arrays):
    return lax.optimization_barrier(arrays)


def gather(w, shard):
    above = lambda a: hop(a, "z", NZ, 1)
    below = lambda a: hop(a, "z", NZ, 7)
    at_first = lax.axis_index("core") == 0
    x = lax.axis_index("x")
    x_t = lax.all_gather(shard, ("y", "core"), axis=0, tiled=True)
    w, part = together(lax.all_gather(w, "x", axis=0, tiled=True), shard)

    first, second = part[:, :L], part[:, L:]
    keep = jnp.where(at_first, first, second)
    come = hop(jnp.where(at_first, second, first), "core", NC, 1)
    v1, e1, come = together(above(w), below(w), come)

    pair = jnp.where(at_first, jnp.concatenate([keep, come], 0), jnp.concatenate([come, keep], 0))
    owned = lax.all_to_all(pair.reshape(NX, ROWS, L), "x", 0, 0)
    v2, e2, x_t, owned = together(above(v1), below(e1), x_t, owned)
    owned = jnp.stack([lax.dynamic_index_in_dim(owned, lax.rem(x + j, NX), 0, False) for j in range(1, NX)])
    owned = lax.all_gather(owned, ("y", "core"), axis=0)

    v3, e3 = together(above(v2), below(e2))
    place = jnp.stack([lax.axis_index(a) for a in ("y", "core", "x", "z")]).astype(jnp.int32)
    x_tok, gram, own = arrange(place, x_t)
    v3, e3, gram = together(v3, e3, gram)
    far = [above(v3[:SHARD]), below(e3[SHARD:])]
    total = project(x_tok, [w, v1, v2, v3, e3, e2])
    owned = owned.reshape(NY, NC, NX - 1, ROWS, L)
    return total, x_tok, [e1, *far], gram, own, owned, place


def body(inputs, w_query, w_key, w_value, cotangent, lengths, sampled, step, tree_noise):
    w = jnp.concatenate([w_query, w_key, w_value], 1)
    total, x_tok, w, gram, own, owned, place = gather(w, inputs.T)

    cosine, sine = rope_tables(L, HD)
    grads, norms = attend(
        jnp.concatenate([lengths, sampled]), total, x_tok, w, cotangent, cosine, sine, gram
    )
    grads = [grads] + [hop(grads, "x", NX, k) for k in range(1, NX)]
    norms, owned = together(lax.psum(norms, "core"), owned)
    norms = lax.all_to_all(jnp.broadcast_to(norms, (NX * NY, 4, HD)), ("x", "y"), 0, 0)
    terms = gradient(place, norms.reshape(NX, NY, 4, HD), stage(owned), own, grads)
    terms = lax.all_to_all(terms, "z", 0, 0)
    summed = jnp.sum(terms.astype(F32), 0)

    levels = tree_noise.shape[0]
    bits = (step[0] // 2 ** jnp.arange(levels, dtype=jnp.int32) % 2).astype(F32)
    noise = jnp.sum(bits[:, None, None, None] * tree_noise, 0)
    expected = 0.85 * (2 * NZ * NX)
    return summed[:, :HD] / expected + noise[0], summed[:, HD:] / expected + noise[1]


def solution(mesh):
    mesh = Mesh(np.asarray(mesh.devices).reshape(NZ, NX, NY, NC), ("z", "x", "y", "core"))
    dp, head = ("z", "x"), ("y", "core")
    in_specs = (
        P(dp, head),
        P(dp, head),
        P(dp, head),
        P(dp, head),
        P(dp, head),
        P(dp),
        P(dp),
        P(),
        P(None, None, dp, head),
    )
    out_specs = (P(dp, head), P(dp, head))
    return jax.shard_map(body, mesh=mesh, in_specs=in_specs, out_specs=out_specs, check_vma=False)
```
